128 devices in a mesh: freq: 4 (over z), rows: 32 (over y, x, core).
Axes of the slice: x: 4, y: 4, z: 4, core: 2. Of those that a mesh axis runs over, the one named last changes fastest.
Arguments:
- histories: float32 [128, 1024, 256], P(('freq', 'rows')), may hold values from -6 to 6
- shift_real: float32 [512], P('freq'), may hold values from 1.5 to 3
- shift_imag: float32 [512], P('freq'), may hold values from -2 to 2
- near_tiles: bfloat16 [4, 64, 8, 512, 512], P('freq', 'rows'), may hold values from -0.09375 to 0.09375
- near_columns: int32 [64, 8], P('rows'), may hold values from 0 to 63, as said below
- left_factors: bfloat16 [4, 2048, 32, 512], P('freq', 'rows'), may hold values from -0.25 to 0.25
- column_factor_tiles: bfloat16 [4, 2048, 32, 512], P('freq', 'rows'), may hold values from -0.25 to 0.25
- tile_rows: int32 [2048], P('rows'), may hold values from 0 to 63, as said below
- tile_cols: int32 [2048], P('rows'), may hold values from 0 to 63
- tile_counts: int32 [32], P('rows'), may hold values from 8 to 64, as said below
Outputs:
- solution: float32 [2, 512, 32768], P(None, 'freq', 'rows')
- residual: float32 [2, 512, 32768], P(None, 'freq', 'rows')
The draws below stay inside these ranges and needn't reach their ends.
Inputs may be any that keep to these rules, and one draw needn't show every extreme that they name: `near_columns`: row i starts with cluster i itself, followed by 8 - 1 other distinct clusters. `tile_rows`: the slots r * 64 to (r + 1) * 64 - 1 name cluster rows r * 2 to (r + 1) * 2 - 1. `tile_counts`: slots past a row block's count are unused; some row block uses all 64 slots.
All inputs are finite; a program needn't handle non-finite values.
Results may differ from the reference program's by a relative error of at most 0.0085.
Values may be sent and summed in bfloat16 or wider, within the bound.
No kernel may reach another device: no remote copies, remote signals or barrier semaphores. Data moves between devices by JAX's collectives and lax.ppermute only.
A program may use at most 192 MiB of HBM per device.

```python
import math
import jax
import jax.numpy as jnp
from jax import lax

STEPS = 1024
FB_DEV = 128
BS = 512
NEAR = 8
RANK = 32
LR_MAX = 64
FREQS = 512
P_SIZE = 32768
NB_DEV = 2
BLOCKS = 64
SLOTS = 2048
SHARE = 256
N_FREQ = 4
N_ROWS = 32


def draw_near_columns(key, part):
    key = jax.random.fold_in(key, 11)
    row_keys = jax.random.split(key, BLOCKS)
    offsets = jax.vmap(lambda row_key: jax.random.permutation(row_key, BLOCKS - 1)[:NEAR - 1] + 1)(row_keys)
    own_rows = jnp.arange(BLOCKS, dtype=jnp.int32)[:, None]
    others = ((own_rows + offsets) % BLOCKS).astype(jnp.int32)
    return jnp.concatenate([own_rows, others], axis=1)


def draw_tile_rows(key, part):
    key = jax.random.fold_in(key, 12)
    owner = jnp.arange(SLOTS, dtype=jnp.int32) // LR_MAX
    return owner * NB_DEV + jax.random.randint(key, (SLOTS,), 0, NB_DEV, dtype=jnp.int32)


def draw_tile_counts(key, part):
    key = jax.random.fold_in(key, 13)
    count_key, order_key = jax.random.split(key)
    lowest = LR_MAX // 8
    counts = jax.random.randint(count_key, (N_ROWS,), lowest, LR_MAX // 2 + 1, dtype=jnp.int32)
    order = jax.random.permutation(order_key, N_ROWS)
    counts = counts.at[order[0]].set(LR_MAX)
    return counts.at[order[1]].set(lowest)


def plant(array, own_key, low, largest):
    place = [jax.random.randint(jax.random.fold_in(own_key, axis), (), 0, length) for axis, length in enumerate(array.shape)]
    longest = array.shape.index(max(array.shape))
    beside = place[:longest] + [(place[longest] + 1) % array.shape[longest]] + place[longest + 1:]
    return array.at[tuple(place)].set(low).at[tuple(beside)].set(largest)


def block_scale(own_key, dims, cuts, smallest, largest):
    level, own = 1.0, jax.random.fold_in(own_key, 6)
    for position, shards_of in cuts:
        heights = jnp.exp(jax.random.uniform(jax.random.fold_in(own, position), (shards_of,), jnp.float32, smallest / len(cuts), largest / len(cuts)))
        level = level * jnp.repeat(heights, dims[position] // shards_of).reshape([-1 if axis == position else 1 for axis in range(len(dims))])
    return level


def noise(rng, shape, spread, bound, cuts=(), kind=jnp.bfloat16):
    loudness = block_scale(rng, shape, cuts, -0.22, 0.18) if cuts else 1.0
    entries = jax.random.normal(rng, shape, jnp.float32) * spread * loudness
    return jnp.minimum(jnp.maximum(entries, -bound), bound).astype(kind)


def setup_inputs(seed: int = 0) -> dict:
    arg_keys = jax.random.split(jax.random.key(seed), 11)
    return {
        "histories": noise(arg_keys[0], (N_FREQ * N_ROWS, STEPS, SHARE), 1.0, 6.0, ((0, 128),), jnp.float32),
        "shift_real": jnp.clip(jnp.exp(math.log(3.0) - 0.6931472 * jax.random.uniform(arg_keys[1], (FREQS,), jnp.float32) ** block_scale(arg_keys[1], (FREQS,), ((0, 4),), -0.2, 0.2)), 1.5, 3.0),
        "shift_imag": jnp.clip(jax.random.uniform(arg_keys[2], (FREQS,), jnp.float32, -2.0, 2.0) * block_scale(arg_keys[2], (FREQS,), ((0, 4),), -0.4, 0.0), -2.0, 2.0),
        "near_tiles": noise(arg_keys[3], (N_FREQ, BLOCKS, NEAR, BS, BS), (NEAR * BS) ** -0.5, 0.09375, ((0, 4), (1, 32))),
        "near_columns": draw_near_columns(jax.random.fold_in(arg_keys[10], 71), 0),
        "left_factors": noise(arg_keys[5], (N_FREQ, SLOTS, RANK, BS), (RANK * 16) ** -0.5, 0.25, ((0, 4), (1, 32))),
        "column_factor_tiles": noise(arg_keys[6], (N_FREQ, SLOTS, RANK, BS), BS ** -0.5, 0.25, ((0, 4), (1, 32))),
        "tile_rows": draw_tile_rows(jax.random.fold_in(arg_keys[10], 71), 0),
        "tile_cols": plant(jax.random.randint(arg_keys[8], (SLOTS,), 0, BLOCKS), jax.random.fold_in(arg_keys[8], 1), 0, BLOCKS - 1).astype(jnp.int32),
        "tile_counts": draw_tile_counts(jax.random.fold_in(arg_keys[10], 71), 0),
    }


damping = 2.0
topmost_precision = lax.Precision.HIGHEST

def dft_table(step_count, freq_count):
    step_index = jnp.arange(step_count, dtype=jnp.int32)
    freq_index = jnp.arange(freq_count, dtype=jnp.int32)
    angles = (freq_index[:, None] * step_index[None, :] % step_count).astype(jnp.float32) * (2.0 * math.pi / step_count)
    weight = jnp.exp(-damping * step_index.astype(jnp.float32) / step_count) * (2.0 / math.sqrt(step_count))
    return (jnp.cos(angles) * weight[None, :], -jnp.sin(angles) * weight[None, :])

def complex_divide(part_real, part_imag, shift_r, shift_i):
    modulus = shift_r * shift_r + shift_i * shift_i
    return ((part_real * shift_r + part_imag * shift_i) / modulus, (part_imag * shift_r - part_real * shift_i) / modulus)

def apply_kernel(dens_real, dens_imag, near_tiles, near_columns, left_factors, column_factor_tiles, tile_rows, tile_cols, tile_counts):
    usable = (jnp.arange(SLOTS, dtype=jnp.int32) % LR_MAX < jnp.repeat(tile_counts, LR_MAX)).astype(jnp.float32)
    outputs = []
    for freq_band in range(N_FREQ):
        first_freq = freq_band * FB_DEV
        stacked = jnp.stack([dens_real[first_freq:first_freq + FB_DEV], dens_imag[first_freq:first_freq + FB_DEV]])
        stacked = stacked.reshape(2 * FB_DEV, BLOCKS, BS).astype(jnp.float32)

        def near_row(row_block):
            near_block = near_tiles[freq_band, row_block].astype(jnp.float32)
            selected_entries = jnp.take(stacked, near_columns[row_block], axis=1)
            return jnp.einsum('krs,cks->cr', near_block, selected_entries)
        near_part = jnp.transpose(lax.map(near_row, jnp.arange(BLOCKS, dtype=jnp.int32)), (1, 0, 2))

        def add_slot(running, slot_index):
            column = lax.dynamic_index_in_dim(stacked, tile_cols[slot_index], 1, keepdims=False)
            right_tile = lax.dynamic_index_in_dim(column_factor_tiles[freq_band], slot_index, 0, keepdims=False).astype(jnp.float32)
            left_tile = lax.dynamic_index_in_dim(left_factors[freq_band], slot_index, 0, keepdims=False).astype(jnp.float32)
            coeffs = jnp.einsum('cs,rs->cr', column, right_tile).astype(jnp.bfloat16)
            coeffs = lax.optimization_barrier(coeffs).astype(jnp.float32)
            contrib = jnp.einsum('cr,rs->cs', coeffs, left_tile) * usable[slot_index]
            target = tile_rows[slot_index]
            current = lax.dynamic_index_in_dim(running, target, 1, keepdims=False)
            return (lax.dynamic_update_index_in_dim(running, current + contrib, target, 1), None)
        low_part, _ = lax.scan(add_slot, jnp.zeros((2 * FB_DEV, BLOCKS, BS), jnp.float32), jnp.arange(SLOTS, dtype=jnp.int32))
        outputs.append((near_part + low_part).reshape(2, FB_DEV, P_SIZE))
    combined = jnp.concatenate(outputs, axis=1)
    return (combined[0], combined[1])

def reference(histories, shift_real, shift_imag, near_tiles, near_columns, left_factors, column_factor_tiles, tile_rows, tile_cols, tile_counts):
    flat_hist = jnp.transpose(histories, (1, 2, 0)).reshape(STEPS, P_SIZE)
    cos_table, sin_table = dft_table(STEPS, FREQS)
    spec_real = jnp.dot(cos_table, flat_hist, precision=topmost_precision).astype(jnp.bfloat16).astype(jnp.float32)
    spec_imag = jnp.dot(sin_table, flat_hist, precision=topmost_precision).astype(jnp.bfloat16).astype(jnp.float32)
    shift_r = shift_real[:, None]
    shift_i = shift_imag[:, None]
    first_real, first_imag = complex_divide(spec_real, spec_imag, shift_r, shift_i)
    first_real = first_real.astype(jnp.bfloat16)
    first_imag = first_imag.astype(jnp.bfloat16)
    kernel_real, kernel_imag = apply_kernel(first_real, first_imag, near_tiles, near_columns, left_factors, column_factor_tiles, tile_rows, tile_cols, tile_counts)
    fixed_real = first_real.astype(jnp.float32)
    settled_imaginary = first_imag.astype(jnp.float32)
    resid_real = spec_real - (shift_r * fixed_real - shift_i * settled_imaginary) - kernel_real
    resid_imag = spec_imag - (shift_r * settled_imaginary + shift_i * fixed_real) - kernel_imag
    corr_real, corr_imag = complex_divide(resid_real, resid_imag, shift_r, shift_i)
    corr_real = corr_real.astype(jnp.bfloat16)
    corr_imag = corr_imag.astype(jnp.bfloat16)
    second_real, second_imag = apply_kernel(corr_real, corr_imag, near_tiles, near_columns, left_factors, column_factor_tiles, tile_rows, tile_cols, tile_counts)
    cfix_real = corr_real.astype(jnp.float32)
    cfix_imag = corr_imag.astype(jnp.float32)
    solution = jnp.stack([fixed_real + cfix_real, settled_imaginary + cfix_imag])
    residual = jnp.stack([resid_real - (shift_r * cfix_real - shift_i * cfix_imag) - second_real, resid_imag - (shift_r * cfix_imag + shift_i * cfix_real) - second_imag])
    return (solution, residual)
```

```python
import functools
import math

import jax
import jax.numpy as jnp
import ml_dtypes
import numpy as np
from jax import lax
from jax.experimental import pallas as pl
from jax.experimental.pallas import tpu as pltpu
from jax.sharding import PartitionSpec as P

STEPS = 1024
FB = 128
BS = 512
NEAR = 8
RANK = 32
SLOTS_HERE = 64
BLOCKS = 64
N_FREQ = 4
N_ROWS = 32
SHARE = 256
W = 2 * FB
NB = 8
damping = 2.0
F32 = jnp.float32
BF16 = jnp.bfloat16


def tables():
    t = np.arange(STEPS, dtype=np.int64)
    f = np.arange(N_FREQ * FB, dtype=np.int64)
    ang = (t[:, None] * f[None, :] % STEPS).astype(np.float64) * (2.0 * math.pi / STEPS)
    weight = (np.exp(-damping * t / STEPS) * (2.0 / math.sqrt(STEPS)))[:, None]
    both = np.stack([np.cos(ang) * weight, -np.sin(ang) * weight], axis=1)
    both = both.reshape(STEPS, 2, N_FREQ, FB).transpose(2, 0, 1, 3).reshape(N_FREQ, STEPS, W)
    both = both.astype(np.float32)
    hi = both.astype(ml_dtypes.bfloat16)
    lo = (both - hi.astype(np.float32)).astype(ml_dtypes.bfloat16)
    return hi, lo


def panel_orders():
    r, z, a = np.meshgrid(np.arange(N_ROWS), np.arange(N_FREQ), np.arange(4), indexing="ij")
    natural = (a * 128 + z * N_ROWS + r).reshape(-1)
    pm = np.zeros((BS, BS), np.float32)
    pm[natural, np.arange(BS)] = 1.0
    em = np.zeros((N_FREQ, 4 * SHARE, SHARE), np.float32)
    j = np.arange(SHARE)
    for zz in range(N_FREQ):
        em[zz, (j // 4) * 16 + zz * 4 + j % 4, j] = 1.0
    return pm.astype(ml_dtypes.bfloat16), em.astype(ml_dtypes.bfloat16)


def dot(a, b):
    return jnp.dot(a, b, preferred_element_type=F32)


def spectrum_kernel(hist_ref, hi_ref, lo_ref, out_ref, thi, tlo):
    @pl.when(pl.program_id(0) == 0)
    def _():
        h = hist_ref[...].T
        hh = h.astype(BF16)
        thi[...] = hh
        tlo[...] = (h - hh.astype(F32)).astype(BF16)

    a, b = thi[...], tlo[...]
    out_ref[0] = (dot(a, hi_ref[0]) + (dot(a, lo_ref[0]) + dot(b, hi_ref[0]))).astype(BF16)


def spectrum(hist, hi, lo):
    return pl.pallas_call(
        spectrum_kernel,
        grid=(N_FREQ,),
        out_shape=jax.ShapeDtypeStruct((N_FREQ, SHARE, W), BF16),
        in_specs=[
            pl.BlockSpec((STEPS, SHARE), lambda b: (0, 0)),
            pl.BlockSpec((1, STEPS, W), lambda b: (b, 0, 0)),
            pl.BlockSpec((1, STEPS, W), lambda b: (b, 0, 0)),
        ],
        out_specs=pl.BlockSpec((1, SHARE, W), lambda b: (b, 0, 0)),
        scratch_shapes=[pltpu.VMEM((SHARE, STEPS), BF16), pltpu.VMEM((SHARE, STEPS), BF16)],
        compiler_params=pltpu.CompilerParams(vmem_limit_bytes=24 << 20),
        name="spectrum",
    )(hist, hi, lo)


def regroup_kernel(em_ref, y_ref, out_ref):
    total = dot(em_ref[0], y_ref[0])
    for z in range(1, N_FREQ):
        total += dot(em_ref[z], y_ref[z])
    out_ref[...] = total.astype(BF16)


def regroup(em, pieces):
    return pl.pallas_call(
        regroup_kernel,
        out_shape=jax.ShapeDtypeStruct((4 * SHARE, W), BF16),
        compiler_params=pltpu.CompilerParams(vmem_limit_bytes=24 << 20),
        name="regroup",
    )(em, pieces)


def operator_kernel(first, ncol, tcol, trow, cnt, vec, dens, near, colf, left_t, *rest):
    if first:
        (pm, first_out, res_out, corr_out,
         gbuf, nbuf, cbuf, lbuf, acc, coef, pbuf, spec, gsem, nsem, csem, lsem, psem) = rest
    else:
        (first_in, res_in, corr_in, sol_out, resid_out,
         gbuf, nbuf, cbuf, lbuf, acc, coef, gsem, nsem, csem, lsem) = rest
    half = W // 2
    tiles = 2 * NEAR
    count = cnt[0]
    total = tiles + count

    def swap(x):
        return jnp.concatenate([x[:, half:], x[:, :half]], axis=1)

    def density_copy(c, slot):
        src = dens.at[:, c] if first else dens.at[c]
        return pltpu.make_async_copy(src, gbuf.at[slot], gsem.at[slot])

    def density_start(v):
        near_c = ncol[jnp.minimum(v, tiles - 1)]
        slot_c = tcol[jnp.clip(v - tiles, 0, SLOTS_HERE - 1)]
        density_copy(jnp.where(v < tiles, near_c, slot_c), lax.rem(v, NB)).start()

    def near_copy(t):
        return pltpu.make_async_copy(near.at[t], nbuf.at[t], nsem.at[t])

    if first:
        pcopy = pltpu.make_async_copy(pm, pbuf, psem)
        pcopy.start()
    for v in range(NB):
        density_start(jnp.int32(v))
        near_copy(v).start()
    for t in range(NB, tiles):
        near_copy(t).start()
    ccopy = pltpu.make_async_copy(colf, cbuf, csem)
    ccopy.start()
    lcopy = pltpu.make_async_copy(left_t, lbuf, lsem)
    lcopy.start()
    acc[...] = jnp.zeros_like(acc)
    coef[...] = jnp.zeros_like(coef)
    if first:
        pcopy.wait()

    def arrived(v):
        slot = lax.rem(v, NB)
        density_copy(0, slot).wait()
        return gbuf[slot].reshape(BS, W)

    def onward(v):
        @pl.when(v + NB < total)
        def _():
            density_start(v + NB)

    def near_step(t, carry):
        x = arrived(t)
        near_copy(t).wait()
        row = t // NEAR
        acc[row] += dot(nbuf[t], x)
        if first:
            @pl.when(lax.rem(t, NEAR) == 0)
            def _():
                spec[row] = dot(pbuf[...], x)
        onward(t)
        return carry

    lax.fori_loop(0, tiles, near_step, 0)
    ccopy.wait()

    def slot_step(j, carry):
        x = arrived(tiles + j)
        start = pl.multiple_of(j * RANK, RANK)
        coef[trow[j], pl.ds(start, RANK), :] = dot(cbuf[pl.ds(start, RANK), :], x).astype(BF16)
        onward(tiles + j)
        return carry

    lax.fori_loop(0, count, slot_step, 0)
    lcopy.wait()

    by_a, by_b, s_c, s_d = vec[0:1, :], vec[1:2, :], vec[2:3, :], vec[3:4, :]
    for i in range(2):
        rows = pl.ds(i * BS, BS)
        k = acc[i] + dot(lbuf[...], coef[i])
        if first:
            x = spec[i]
            f16 = (x * by_a + swap(x) * by_b).astype(BF16)
            f = f16.astype(F32)
            res = x - (f * s_c + swap(f) * s_d) - (k * by_a + swap(k) * by_b)
            first_out[rows, :] = f16
            res_out[rows, :] = res
            corr_out[rows, :] = (res * by_a + swap(res) * by_b).astype(BF16)
        else:
            c = corr_in[rows, :].astype(F32)
            sol_out[:, rows] = (first_in[rows, :].astype(F32) + c).T
            resid_out[:, rows] = (res_in[rows, :] - (c * s_c + swap(c) * s_d) - k).T


def operator(first, ncol, tcol, trow, cnt, vec, dens, near, colf, left_t, *extra):
    smem = pl.BlockSpec(memory_space=pltpu.SMEM)
    vmem = pl.BlockSpec(memory_space=pltpu.VMEM)
    hbm = pl.BlockSpec(memory_space=pl.ANY)
    panels = 2 * BS
    gshape = (NB, N_ROWS, BS // N_ROWS, W) if first else (NB, BS, W)
    scratch = [
        pltpu.VMEM(gshape, BF16),
        pltpu.VMEM((2 * NEAR, BS, BS), BF16),
        pltpu.VMEM((SLOTS_HERE * RANK, BS), BF16),
        pltpu.VMEM((BS, SLOTS_HERE * RANK), BF16),
        pltpu.VMEM((2, BS, W), F32),
        pltpu.VMEM((2, SLOTS_HERE * RANK, W), BF16),
    ]
    sems = [
        pltpu.SemaphoreType.DMA((NB,)),
        pltpu.SemaphoreType.DMA((2 * NEAR,)),
        pltpu.SemaphoreType.DMA,
        pltpu.SemaphoreType.DMA,
    ]
    if first:
        scratch += [pltpu.VMEM((BS, BS), BF16), pltpu.VMEM((2, BS, W), F32)]
        sems += [pltpu.SemaphoreType.DMA]
        outs = [
            jax.ShapeDtypeStruct((panels, W), BF16),
            jax.ShapeDtypeStruct((panels, W), F32),
            jax.ShapeDtypeStruct((panels, W), BF16),
        ]
        extra_specs = [hbm]
    else:
        outs = [jax.ShapeDtypeStruct((W, panels), F32)] * 2
        extra_specs = [vmem] * 3
    return pl.pallas_call(
        functools.partial(operator_kernel, first),
        out_shape=outs,
        in_specs=[smem] * 4 + [vmem] + [hbm] * 4 + extra_specs,
        out_specs=[vmem] * len(outs),
        scratch_shapes=scratch + sems,
        compiler_params=pltpu.CompilerParams(vmem_limit_bytes=48 << 20),
        name="operator_first" if first else "operator_second",
    )(ncol, tcol, trow, cnt, vec, dens, near, colf, left_t, *extra)


def body(consts, histories, shift_real, shift_imag, near_tiles, near_columns, left_factors,
         column_factor_tiles, tile_rows, tile_cols, tile_counts):
    hi, lo, pm, em = consts
    row_start = lax.axis_index("rows") * 2
    modulus = shift_real * shift_real + shift_imag * shift_imag
    inv_r, inv_i = shift_real / modulus, shift_imag / modulus
    vec = jnp.stack([
        jnp.concatenate([inv_r, inv_r]),
        jnp.concatenate([inv_i, -inv_i]),
        jnp.concatenate([shift_real, shift_real]),
        jnp.concatenate([-shift_imag, shift_imag]),
    ])
    near = near_tiles.reshape(2 * NEAR, BS, BS)
    colf = column_factor_tiles.reshape(SLOTS_HERE * RANK, BS)
    left_t = left_factors.reshape(SLOTS_HERE * RANK, BS).T
    scalars = (near_columns.reshape(-1), tile_cols, tile_rows - row_start, tile_counts, vec)

    spec = spectrum(histories[0], hi, lo)
    pieces = lax.all_to_all(spec, "freq", split_axis=0, concat_axis=0)
    block = regroup(em, pieces)
    every = lax.all_gather(block, "rows", axis=0, tiled=False)
    every = every.reshape(N_ROWS, BLOCKS, BS // N_ROWS, W)

    near_p = dot(near.reshape(-1, BS), pm).astype(BF16).reshape(near.shape)
    colf_p = dot(colf, pm).astype(BF16)

    fixed, resid, corr = operator(True, *scalars, every, near_p, colf_p, left_t, pm)
    corr_all = lax.all_gather(corr, "rows", axis=0, tiled=False).reshape(BLOCKS, BS, W)
    sol, final = operator(False, *scalars, corr_all, near, colf, left_t, fixed, resid, corr)
    return sol.reshape(2, FB, 2 * BS), final.reshape(2, FB, 2 * BS)


def solution(mesh):
    hi, lo = tables()
    pm, em = panel_orders()
    placed = (
        P(("freq", "rows"), None, None),
        P("freq"),
        P("freq"),
        P("freq", "rows", None, None, None),
        P("rows", None),
        P("freq", "rows", None, None),
        P("freq", "rows", None, None),
        P("rows"),
        P("rows"),
        P("rows"),
    )

    def run(*args):
        consts = tuple(jnp.asarray(c) for c in (hi, lo, pm, em))
        return jax.shard_map(
            body,
            mesh=mesh,
            in_specs=((P(), P(), P(), P()),) + placed,
            out_specs=(P(None, "freq", "rows"), P(None, "freq", "rows")),
            check_vma=False,
        )(consts, *args)

    return run
```

```python
import functools
import math

import jax
import jax.numpy as jnp
import ml_dtypes
import numpy as np
from jax import lax
from jax.experimental import pallas as pl
from jax.experimental.pallas import tpu as pltpu
from jax.sharding import PartitionSpec as P

STEPS = 1024
FB = 128
BS = 512
NEAR = 8
RANK = 32
SLOTS_HERE = 64
BLOCKS = 64
N_FREQ = 4
N_ROWS = 32
SHARE = 256
W = 2 * FB
HALF = FB // 2
L = 2 * HALF
CHIPS = 16
damping = 2.0
F32 = jnp.float32
BF16 = jnp.bfloat16


def tables():
    t = np.arange(STEPS, dtype=np.int64)
    f = np.arange(N_FREQ * FB, dtype=np.int64)
    ang = (t[:, None] * f[None, :] % STEPS).astype(np.float64) * (2.0 * math.pi / STEPS)
    weight = (np.exp(-damping * t / STEPS) * (2.0 / math.sqrt(STEPS)))[:, None]
    both = np.stack([np.cos(ang) * weight, -np.sin(ang) * weight], axis=1)
    both = both.reshape(STEPS, 2, N_FREQ, 2, HALF).transpose(2, 0, 3, 1, 4).reshape(N_FREQ, STEPS, W)
    both = both.astype(np.float32)
    hi = both.astype(ml_dtypes.bfloat16)
    lo = (both - hi.astype(np.float32)).astype(ml_dtypes.bfloat16)
    return hi, lo


def regroup_table():
    em = np.zeros((N_FREQ, BS, FB), np.float32)
    j = np.arange(FB)
    for z in range(N_FREQ):
        em[z, (j // 4) * 16 + z * 4 + j % 4, j] = 1.0
    return em.astype(ml_dtypes.bfloat16)


def dot(a, b):
    return jnp.dot(a, b, preferred_element_type=F32)


def spectrum_kernel(core, hist_ref, hi_ref, lo_ref, own_ref, other_ref, thi, tlo):
    @pl.when(pl.program_id(0) == 0)
    def _():
        h = hist_ref[...].T
        hh = h.astype(BF16)
        thi[...] = hh
        tlo[...] = (h - hh.astype(F32)).astype(BF16)

    a, b = thi[...], tlo[...]
    total = (dot(a, hi_ref[0]) + (dot(a, lo_ref[0]) + dot(b, hi_ref[0]))).astype(BF16)
    swapped = core[0] == 1
    own_ref[0] = jnp.where(swapped, total[:, L:], total[:, :L])
    other_ref[0] = jnp.where(swapped, total[:, :L], total[:, L:])


def spectrum(core, hist, hi, lo):
    return pl.pallas_call(
        spectrum_kernel,
        grid=(N_FREQ,),
        out_shape=[jax.ShapeDtypeStruct((N_FREQ, SHARE, L), BF16)] * 2,
        in_specs=[
            pl.BlockSpec(memory_space=pltpu.SMEM),
            pl.BlockSpec((STEPS, SHARE), lambda b: (0, 0)),
            pl.BlockSpec((1, STEPS, W), lambda b: (b, 0, 0)),
            pl.BlockSpec((1, STEPS, W), lambda b: (b, 0, 0)),
        ],
        out_specs=[pl.BlockSpec((1, SHARE, L), lambda b: (b, 0, 0))] * 2,
        scratch_shapes=[pltpu.VMEM((SHARE, STEPS), BF16), pltpu.VMEM((SHARE, STEPS), BF16)],
        compiler_params=pltpu.CompilerParams(vmem_limit_bytes=24 << 20),
        cost_estimate=pl.CostEstimate(flops=2_000_000_000, bytes_accessed=6 << 20, transcendentals=0),
        name="spectrum",
    )(core, hist, hi, lo)


def regroup_kernel(em_ref, y_ref, p_ref, q_ref):
    for cc in range(2):
        for out, start in ((p_ref, 0), (q_ref, FB)):
            total = dot(em_ref[0], y_ref[0, cc, start:start + FB])
            for z in range(1, N_FREQ):
                total += dot(em_ref[z], y_ref[z, cc, start:start + FB])
            out[cc * BS:(cc + 1) * BS, :] = total.astype(BF16)


def regroup(em, pieces):
    return pl.pallas_call(
        regroup_kernel,
        out_shape=[jax.ShapeDtypeStruct((2 * BS, L), BF16)] * 2,
        compiler_params=pltpu.CompilerParams(vmem_limit_bytes=16 << 20),
        name="regroup",
    )(em, pieces)


def reorder_kernel(near_ref, colf_ref, pm_ref, near_out, colf_out):
    near_out[0] = dot(near_ref[0], pm_ref[...]).astype(BF16)
    colf_out[...] = dot(colf_ref[...], pm_ref[...]).astype(BF16)


def reorder(near, colf, pm):
    tiles = 2 * NEAR
    near_spec = pl.BlockSpec((1, BS, BS), lambda t: (t, 0, 0))
    colf_spec = pl.BlockSpec((SLOTS_HERE * RANK // tiles, BS), lambda t: (t, 0))
    return pl.pallas_call(
        reorder_kernel,
        grid=(tiles,),
        out_shape=[jax.ShapeDtypeStruct(near.shape, BF16), jax.ShapeDtypeStruct(colf.shape, BF16)],
        in_specs=[near_spec, colf_spec, pl.BlockSpec((BS, BS), lambda t: (0, 0))],
        out_specs=[near_spec, colf_spec],
        compiler_params=pltpu.CompilerParams(vmem_limit_bytes=16 << 20),
        cost_estimate=pl.CostEstimate(flops=5_000_000_000, bytes_accessed=22 << 20, transcendentals=0),
        name="reorder",
    )(near, colf, pm)


def operator_kernel(first, ncol, tcol, trow, cnt, pos, vec, near, colf, left_t, *rest):
    dens, rest = rest[:10], rest[10:]
    if first:
        (pm, corr_out, res_out, sol_out,
         vm, nbuf, cbuf, lbuf, acc, low, coef, pbuf, spec, gsem, nsem, csem, lsem, psem) = rest
    else:
        (corr_in, res_in, resid_out,
         vm, nbuf, cbuf, lbuf, acc, low, coef, gsem, nsem, csem, lsem) = rest
    tiles = 2 * NEAR
    group = 8
    count = cnt[0]

    def swap(x):
        return pltpu.roll(x, HALF, 1)

    copies = []
    for s in range(2):
        at = 0
        for k, chips in enumerate((4, 4, 4, 2, 2)):
            if first:
                dst = vm.at[s, pl.ds(at, chips)]
            else:
                dst = vm.at[pl.ds((s * CHIPS + at) * 2, chips * 2)]
            copies.append(pltpu.make_async_copy(dens[5 * s + k], dst, gsem.at[5 * s + k]))
            at += chips

    def near_copy(t):
        return pltpu.make_async_copy(near.at[t], nbuf.at[t], nsem.at[t])

    for copy in copies:
        copy.start()
    for t in range(4):
        near_copy(t).start()
    if first:
        pcopy = pltpu.make_async_copy(pm, pbuf, psem)
        pcopy.start()
    for t in range(4, tiles):
        near_copy(t).start()
    ccopy = pltpu.make_async_copy(colf, cbuf, csem)
    ccopy.start()
    lcopy = pltpu.make_async_copy(left_t, lbuf, lsem)
    lcopy.start()
    acc[...] = jnp.zeros_like(acc)
    low[...] = jnp.zeros_like(low)
    for copy in copies:
        copy.wait()

    def panels(c):
        if first:
            return vm[lax.div(c, 32), :, :, lax.rem(c, 32)].reshape(BS, L)
        return vm[pos[c]]

    def near_step(g, carry):
        i = lax.div(g, 2)
        total = acc[i]
        for u in range(4):
            t = g * 4 + u
            near_copy(t).wait()
            total += dot(nbuf[t], panels(ncol[t]))
        acc[i] = total
        return carry

    lax.fori_loop(0, tiles // 4, near_step, 0)
    if first:
        pcopy.wait()
        for i in range(2):
            spec[i] = dot(pbuf[...], panels(ncol[i * NEAR]))
    ccopy.wait()
    lcopy.wait()

    def slot_step(g, carry):
        base = pl.multiple_of(g * (group * RANK), group * RANK)
        for u in range(group):
            j = g * group + u
            rows = pl.ds(pl.multiple_of(base + u * RANK, RANK), RANK)
            val = dot(cbuf[rows, :], panels(tcol[j]))
            used = j < count
            for i in range(2):
                mask = jnp.where(used & (trow[j] == i), 1.0, 0.0).astype(F32)
                coef[u * RANK:(u + 1) * RANK, i * L:(i + 1) * L] = (val * mask).astype(BF16)
        low[...] += dot(lbuf[:, pl.ds(base, group * RANK)], coef[...])
        return carry

    lax.fori_loop(0, lax.div(count + group - 1, group), slot_step, 0)

    by_a, by_b, s_c, s_d = vec[0:1, :], vec[1:2, :], vec[2:3, :], vec[3:4, :]
    for i in range(2):
        rows = slice(i * BS, (i + 1) * BS)
        k = acc[i] + low[:, i * L:(i + 1) * L]
        if first:
            x = spec[i]
            f = (x * by_a + swap(x) * by_b).astype(BF16).astype(F32)
            res = x - (f * s_c + swap(f) * s_d) - (k * by_a + swap(k) * by_b)
            corr = (res * by_a + swap(res) * by_b).astype(BF16)
            corr_out[rows, :] = corr
            res_out[rows, :] = res
            sol_out[:, rows] = (f + corr.astype(F32)).T
        else:
            c = corr_in[rows, :].astype(F32)
            resid_out[:, rows] = (res_in[rows, :] - (c * s_c + swap(c) * s_d) - k).T


def operator(first, scalars, tables, dens, *extra):
    smem = pl.BlockSpec(memory_space=pltpu.SMEM)
    vmem = pl.BlockSpec(memory_space=pltpu.VMEM)
    hbm = pl.BlockSpec(memory_space=pl.ANY)
    panels = 2 * BS
    vshape = (2, CHIPS, 2, 32, 16, L) if first else (4 * CHIPS, BS, L)
    block = (2, 32, 16, L) if first else (BS, L)
    per_chip = 1 if first else 2
    dens = [d.reshape((d.shape[0] * per_chip // panels,) + block) for d in dens]
    scratch = [
        pltpu.VMEM(vshape, BF16),
        pltpu.VMEM((2 * NEAR, BS, BS), BF16),
        pltpu.VMEM((SLOTS_HERE * RANK, BS), BF16),
        pltpu.VMEM((BS, SLOTS_HERE * RANK), BF16),
        pltpu.VMEM((2, BS, L), F32),
        pltpu.VMEM((BS, 2 * L), F32),
        pltpu.VMEM((8 * RANK, 2 * L), BF16),
    ]
    sems = [
        pltpu.SemaphoreType.DMA((10,)),
        pltpu.SemaphoreType.DMA((2 * NEAR,)),
        pltpu.SemaphoreType.DMA,
        pltpu.SemaphoreType.DMA,
    ]
    turned = jax.ShapeDtypeStruct((L, panels), F32)
    if first:
        scratch += [pltpu.VMEM((BS, BS), BF16), pltpu.VMEM((2, BS, L), F32)]
        sems += [pltpu.SemaphoreType.DMA]
        outs = [jax.ShapeDtypeStruct((panels, L), BF16), jax.ShapeDtypeStruct((panels, L), F32), turned]
        extra_specs = [hbm]
    else:
        outs = [turned]
        extra_specs = [vmem] * 2
    return pl.pallas_call(
        functools.partial(operator_kernel, first),
        out_shape=outs,
        in_specs=[smem] * 5 + [vmem] + [hbm] * 13 + extra_specs,
        out_specs=[vmem] * len(outs),
        scratch_shapes=scratch + sems,
        compiler_params=pltpu.CompilerParams(vmem_limit_bytes=30 << 20),
        cost_estimate=pl.CostEstimate(flops=6_000_000_000, bytes_accessed=21 << 20, transcendentals=0),
        name="operator_first" if first else "operator_second",
    )(*scalars, *tables, *dens, *extra)


def index_of(y, x, core):
    return ((y % 4) * 4 + x % 4) * 2 + core


def step_pairs(stage, shift):
    pairs = []
    for y in range(4):
        for x in range(4):
            for core in range(2):
                along_x = (stage == 0) == (core == 0)
                target = index_of(y, x + shift, core) if along_x else index_of(y + shift, x, core)
                pairs.append((index_of(y, x, core), target))
    return pairs


def shifted(v, stage, shift):
    return lax.ppermute(v, "rows", step_pairs(stage, shift))


def to_other_core(v):
    return lax.ppermute(v, "rows", [(i, i ^ 1) for i in range(N_ROWS)])


def gather_chips(v):
    n = v.shape[0]
    before, after, across = shifted(v, 0, 1), shifted(v, 0, -1), shifted(v, 0, 2)
    line = jnp.concatenate([v, before, after, across], 0)
    line_before, line_after = shifted(line, 1, 1), shifted(line, 1, -1)
    across_lo = shifted(line_before[:2 * n], 1, 1)
    across_hi = shifted(line_after[2 * n:], 1, -1)
    return [line, line_before, line_after, across_lo, across_hi]


def body(consts, histories, shift_real, shift_imag, near_tiles, near_columns, left_factors,
         column_factor_tiles, tile_rows, tile_cols, tile_counts):
    hi, lo, em = consts
    me = lax.axis_index("rows")
    core, x0, y0 = me % 2, (me // 2) % 4, me // 8

    def own_half(s):
        return jnp.where(core == 0, s[:HALF], s[HALF:])

    shift_r, shift_i = own_half(shift_real), own_half(shift_imag)
    modulus = shift_r * shift_r + shift_i * shift_i
    inv_r, inv_i = shift_r / modulus, shift_i / modulus
    vec = jnp.stack([
        jnp.concatenate([inv_r, inv_r]),
        jnp.concatenate([inv_i, -inv_i]),
        jnp.concatenate([shift_r, shift_r]),
        jnp.concatenate([-shift_i, shift_i]),
    ])

    place_of = jnp.array([0, 2, 3, 1], jnp.int32)
    offset_of = jnp.array([0, 3, 1, 2], jnp.int32)
    clusters = jnp.arange(BLOCKS, dtype=jnp.int32)
    to_x, to_y = place_of[(clusters // 4 - x0) % 4], place_of[(clusters // 16 - y0) % 4]
    chip_place = jnp.where(core == 0, to_y * 4 + to_x, to_x * 4 + to_y)
    pos = ((((clusters // 2) % 2) ^ core) * CHIPS + chip_place) * 2 + clusters % 2
    s = jnp.arange(BS, dtype=jnp.int32)
    major, minor = offset_of[s // 128], offset_of[(s // 32) % 4]
    from_x, from_y = jnp.where(core == 0, minor, major), jnp.where(core == 0, major, minor)
    row_device = (((y0 + from_y) % 4) * 4 + (x0 + from_x) % 4) * 2 + (((s // 16) % 2) ^ core)
    natural = (s % 4) * 128 + ((s // 4) % 4) * N_ROWS + row_device
    pm = (s[:, None] == natural[None, :]).astype(BF16)

    near = near_tiles.reshape(2 * NEAR, BS, BS)
    colf = column_factor_tiles.reshape(SLOTS_HERE * RANK, BS)
    left_t = left_factors.reshape(SLOTS_HERE * RANK, BS).T
    whole = jnp.concatenate([near_columns.reshape(-1), tile_cols, tile_rows - me * 2, tile_counts])
    whole_s = to_other_core(whole)
    near_s, colf_s, left_s = to_other_core(near), to_other_core(colf), to_other_core(left_t)

    def scalars_of(w):
        return (w[:16], w[16:80], w[80:144], w[144:145], pos, vec)

    scalars, scalars_s = scalars_of(whole), scalars_of(whole_s)

    own, other = spectrum(core.reshape(1), histories[0], hi, lo)
    sent = to_other_core(other)
    pieces = lax.all_to_all(jnp.stack([own, sent], axis=1), "freq", split_axis=0, concat_axis=0)
    block_p, block_q = regroup(em, pieces)
    every = gather_chips(block_p) + gather_chips(block_q)

    near_p, colf_p = reorder(near, colf, pm)
    near_ps, colf_ps = reorder(near_s, colf_s, pm)

    corr, res, sol = operator(True, scalars, (near_p, colf_p, left_t), every, pm)
    corr_s, res_s, sol_s = operator(True, scalars_s, (near_ps, colf_ps, left_s), every, pm)
    every = gather_chips(corr) + gather_chips(corr_s)
    sol_got = to_other_core(sol_s)
    (resid_s,) = operator(False, scalars_s, (near_s, colf_s, left_s), every, corr_s, res_s)
    resid_got = to_other_core(resid_s)
    (resid,) = operator(False, scalars, (near, colf, left_t), every, corr, res)

    def assemble(mine, got):
        mine, got = mine.reshape(2, 1, HALF, 2 * BS), got.reshape(2, 1, HALF, 2 * BS)
        low, high = jnp.where(core == 0, mine, got), jnp.where(core == 0, got, mine)
        return jnp.concatenate([low, high], axis=1).reshape(2, FB, 2 * BS)

    return assemble(sol, sol_got), assemble(resid, resid_got)


def solution(mesh):
    hi, lo = tables()
    em = regroup_table()
    placed = (
        P(("freq", "rows"), None, None),
        P("freq"),
        P("freq"),
        P("freq", "rows", None, None, None),
        P("rows", None),
        P("freq", "rows", None, None),
        P("freq", "rows", None, None),
        P("rows"),
        P("rows"),
        P("rows"),
    )

    def run(*args):
        consts = tuple(jnp.asarray(c) for c in (hi, lo, em))
        return jax.shard_map(
            body,
            mesh=mesh,
            in_specs=((P(), P(), P()),) + placed,
            out_specs=(P(None, "freq", "rows"), P(None, "freq", "rows")),
            check_vma=False,
        )(consts, *args)

    return run
```

```python
import functools
import math

import jax
import jax.numpy as jnp
import ml_dtypes
import numpy as np
from jax import lax
from jax.experimental import pallas as pl
from jax.experimental.pallas import tpu as pltpu
from jax.sharding import PartitionSpec as P

STEPS = 1024
FB = 128
BS = 512
NEAR = 8
RANK = 32
SLOTS_HERE = 64
BLOCKS = 64
N_FREQ = 4
N_ROWS = 32
SHARE = 256
W = 2 * FB
HALF = FB // 2
L = 2 * HALF
CHIPS = 16
damping = 2.0
F32 = jnp.float32
BF16 = jnp.bfloat16


def tables():
    t = np.arange(STEPS, dtype=np.int64)
    f = np.arange(N_FREQ * FB, dtype=np.int64)
    ang = (t[:, None] * f[None, :] % STEPS).astype(np.float64) * (2.0 * math.pi / STEPS)
    weight = (np.exp(-damping * t / STEPS) * (2.0 / math.sqrt(STEPS)))[:, None]
    both = np.stack([np.cos(ang) * weight, -np.sin(ang) * weight], axis=1)
    both = both.reshape(STEPS, 2, N_FREQ, 2, HALF).transpose(2, 0, 3, 1, 4).reshape(N_FREQ, STEPS, W)
    both = both.astype(np.float32)
    hi = both.astype(ml_dtypes.bfloat16)
    lo = (both - hi.astype(np.float32)).astype(ml_dtypes.bfloat16)
    return hi, lo


def dot(a, b):
    return jnp.dot(a, b, preferred_element_type=F32)


def spectrum_kernel(hist_ref, hi_ref, lo_ref, out_ref, hbuf, hibuf, lobuf, hsem, hisem, losem):
    hcopy = pltpu.make_async_copy(hist_ref, hbuf, hsem)
    hcopy.start()
    copies = []
    for b in range(N_FREQ):
        pair = (pltpu.make_async_copy(hi_ref.at[b], hibuf.at[b], hisem.at[b]),
                pltpu.make_async_copy(lo_ref.at[b], lobuf.at[b], losem.at[b]))
        copies.append(pair)
        for copy in pair:
            copy.start()
    hcopy.wait()
    h = hbuf[...].T
    hh = h.astype(BF16)
    hl = (h - hh.astype(F32)).astype(BF16)
    for b in range(N_FREQ):
        for copy in copies[b]:
            copy.wait()
        total = dot(hh, hibuf[b]) + (dot(hh, lobuf[b]) + dot(hl, hibuf[b]))
        for c in range(2):
            out_ref[b, :, c] = total[:, c * L:(c + 1) * L].astype(BF16).reshape(CHIPS, 16, L)


def spectrum(hist, hi, lo):
    return pl.pallas_call(
        spectrum_kernel,
        out_shape=jax.ShapeDtypeStruct((N_FREQ, CHIPS, 2, 16, L), BF16),
        in_specs=[pl.BlockSpec(memory_space=pl.ANY)] * 3,
        out_specs=pl.BlockSpec(memory_space=pltpu.VMEM),
        scratch_shapes=[
            pltpu.VMEM((STEPS, SHARE), F32),
            pltpu.VMEM((N_FREQ, STEPS, W), BF16),
            pltpu.VMEM((N_FREQ, STEPS, W), BF16),
            pltpu.SemaphoreType.DMA,
            pltpu.SemaphoreType.DMA((N_FREQ,)),
            pltpu.SemaphoreType.DMA((N_FREQ,)),
        ],
        compiler_params=pltpu.CompilerParams(vmem_limit_bytes=60 << 20),
        cost_estimate=pl.CostEstimate(flops=3_000_000_000, bytes_accessed=6 << 20, transcendentals=0),
        name="spectrum",
    )(hist, hi, lo)


def regroup_kernel(where, in_ref, p_ref, q_ref, wide):
    wide[...] = in_ref[...].astype(F32)
    swapped = where[0] == 1
    for i in range(2):
        for a in range(4):
            low = wide[:, i * 4 + a, :].astype(BF16)
            high = wide[:, 8 + i * 4 + a, :].astype(BF16)
            rows = slice(i * BS + a * 128, i * BS + (a + 1) * 128)
            p_ref[rows, :] = jnp.where(swapped, high, low)
            q_ref[rows, :] = jnp.where(swapped, low, high)


def regroup(where, pieces):
    vmem = pl.BlockSpec(memory_space=pltpu.VMEM)
    return pl.pallas_call(
        regroup_kernel,
        out_shape=[jax.ShapeDtypeStruct((2 * BS, L), BF16)] * 2,
        in_specs=[pl.BlockSpec(memory_space=pltpu.SMEM), vmem],
        out_specs=[vmem] * 2,
        scratch_shapes=[pltpu.VMEM((N_FREQ * N_ROWS, 16, L), F32)],
        compiler_params=pltpu.CompilerParams(vmem_limit_bytes=8 << 20),
        cost_estimate=pl.CostEstimate(flops=0, bytes_accessed=2 << 20, transcendentals=0),
        name="regroup",
    )(where, pieces)


def join_kernel(a, b, c, d, out, sem):
    copies = [pltpu.make_async_copy(ref, out.at[k], sem.at[k]) for k, ref in enumerate((a, b, c, d))]
    for copy in copies:
        copy.start()
    for copy in copies:
        copy.wait()


def join(parts):
    rows, lanes = parts[0].shape
    return pl.pallas_call(
        join_kernel,
        out_shape=jax.ShapeDtypeStruct((4, rows, lanes), BF16),
        in_specs=[pl.BlockSpec(memory_space=pl.ANY)] * 4,
        out_specs=pl.BlockSpec(memory_space=pltpu.VMEM),
        scratch_shapes=[pltpu.SemaphoreType.DMA((4,))],
        compiler_params=pltpu.CompilerParams(vmem_limit_bytes=4 << 20),
        cost_estimate=pl.CostEstimate(flops=0, bytes_accessed=2 << 20, transcendentals=0),
        name="join",
    )(*parts).reshape(4 * rows, lanes)


def operator_kernel(first, load, ncol, tcol, trow, cnt, pos, vec, near, colf, left_t, *rest):
    if load:
        dens, rest = rest[:10], rest[10:]
    else:
        vm, rest = rest[0], rest[1:]
    if first:
        spec, corr_out, res_out, sol_out = rest[:4]
        rest = rest[4:]
    else:
        corr_in, res_in, resid_out = rest[:3]
        rest = rest[3:]
    if load:
        vm, rest = rest[0], rest[1:]
    acc, low, coef, gsem = rest
    tiles = 2 * NEAR
    group = 8
    count = cnt[0]

    def swap(x):
        return pltpu.roll(x, HALF, 1)

    copies = []
    for s in range(2 if load else 0):
        at = 0
        for k, chips in enumerate((4, 4, 4, 2, 2)):
            dst = vm.at[pl.ds((s * CHIPS + at) * 2, chips * 2)]
            copies.append(pltpu.make_async_copy(dens[5 * s + k], dst, gsem.at[5 * s + k]))
            at += chips

    for copy in copies:
        copy.start()
    acc[...] = jnp.zeros_like(acc)
    low[...] = jnp.zeros_like(low)
    for copy in copies:
        copy.wait()

    def panels(c):
        return vm[pos[c]]

    def near_step(g, carry):
        i = lax.div(g, 2)
        total = acc[i]
        for u in range(4):
            t = g * 4 + u
            total += dot(near[t], panels(ncol[t]))
        acc[i] = total
        return carry

    lax.fori_loop(0, tiles // 4, near_step, 0)
    def slot_step(g, carry):
        base = pl.multiple_of(g * (group * RANK), group * RANK)
        for u in range(group):
            j = g * group + u
            rows = pl.ds(pl.multiple_of(base + u * RANK, RANK), RANK)
            val = dot(colf[rows, :], panels(tcol[j]))
            used = j < count
            for i in range(2):
                mask = jnp.where(used & (trow[j] == i), 1.0, 0.0).astype(F32)
                coef[u * RANK:(u + 1) * RANK, i * L:(i + 1) * L] = (val * mask).astype(BF16)
        low[...] += dot(left_t[:, pl.ds(base, group * RANK)], coef[...])
        return carry

    lax.fori_loop(0, lax.div(count + group - 1, group), slot_step, 0)

    by_a, by_b, s_c, s_d = vec[0:1, :], vec[1:2, :], vec[2:3, :], vec[3:4, :]
    for i in range(2):
        rows = slice(i * BS, (i + 1) * BS)
        k = acc[i] + low[:, i * L:(i + 1) * L]
        if first:
            x = spec[rows, :].astype(F32)
            f = (x * by_a + swap(x) * by_b).astype(BF16).astype(F32)
            res = x - (f * s_c + swap(f) * s_d) - (k * by_a + swap(k) * by_b)
            corr = (res * by_a + swap(res) * by_b).astype(BF16)
            corr_out[rows, :] = corr
            res_out[rows, :] = res
            sol_out[:, rows] = (f + corr.astype(F32)).T
        else:
            c = corr_in[rows, :].astype(F32)
            resid_out[:, rows] = (res_in[rows, :] - (c * s_c + swap(c) * s_d) - k).T


def operator(first, load, scalars, tables, dens, *extra):
    smem = pl.BlockSpec(memory_space=pltpu.SMEM)
    vmem = pl.BlockSpec(memory_space=pltpu.VMEM)
    hbm = pl.BlockSpec(memory_space=pl.ANY)
    panels = 2 * BS
    dens = [d.reshape(-1, BS, L) for d in dens]
    scratch = [
        pltpu.VMEM((2, BS, L), F32),
        pltpu.VMEM((BS, 2 * L), F32),
        pltpu.VMEM((8 * RANK, 2 * L), BF16),
        pltpu.SemaphoreType.DMA((10,)),
    ]
    turned = jax.ShapeDtypeStruct((L, panels), F32)
    if first:
        outs = [jax.ShapeDtypeStruct((panels, L), BF16), jax.ShapeDtypeStruct((panels, L), F32), turned]
    else:
        outs = [turned]
    if load:
        outs.append(jax.ShapeDtypeStruct((4 * CHIPS, BS, L), BF16))
    return pl.pallas_call(
        functools.partial(operator_kernel, first, load),
        out_shape=outs,
        in_specs=[smem] * 5 + [vmem] * 4 + ([hbm] * 10 if load else [vmem]) + [vmem] * len(extra),
        out_specs=[vmem] * len(outs),
        scratch_shapes=scratch,
        compiler_params=pltpu.CompilerParams(vmem_limit_bytes=16 << 20),
        cost_estimate=pl.CostEstimate(flops=6_000_000_000, bytes_accessed=21 << 20, transcendentals=0),
        name="operator_first" if first else "operator_second",
    )(*scalars, *tables, *dens, *extra)


def index_of(y, x, core):
    return ((y % 4) * 4 + x % 4) * 2 + core


def step_pairs(stage, shift):
    pairs = []
    for y in range(4):
        for x in range(4):
            for core in range(2):
                along_x = (stage == 0) == (core == 0)
                target = index_of(y, x + shift, core) if along_x else index_of(y + shift, x, core)
                pairs.append((index_of(y, x, core), target))
    return pairs


def shifted(v, stage, shift):
    return lax.ppermute(v, "rows", step_pairs(stage, shift))


def to_other_core(v):
    return lax.ppermute(v, "rows", [(i, i ^ 1) for i in range(N_ROWS)])


def gather_chips(v):
    n = v.shape[0]
    before, after, across = shifted(v, 0, 1), shifted(v, 0, -1), shifted(v, 0, 2)
    line = join([v, before, after, across])
    line_before, line_after = shifted(line, 1, 1), shifted(line, 1, -1)
    across_lo = shifted(line_before[:2 * n], 1, 1)
    across_hi = shifted(line_after[2 * n:], 1, -1)
    return [line, line_before, line_after, across_lo, across_hi]


def body(consts, histories, shift_real, shift_imag, near_tiles, near_columns, left_factors,
         column_factor_tiles, tile_rows, tile_cols, tile_counts):
    hi, lo = consts
    me = lax.axis_index("rows")
    core, x0, y0 = me % 2, (me // 2) % 4, me // 8

    def own_half(s):
        return jnp.where(core == 0, s[:HALF], s[HALF:])

    shift_r, shift_i = own_half(shift_real), own_half(shift_imag)
    modulus = shift_r * shift_r + shift_i * shift_i
    inv_r, inv_i = shift_r / modulus, shift_i / modulus
    vec = jnp.stack([
        jnp.concatenate([inv_r, inv_r]),
        jnp.concatenate([inv_i, -inv_i]),
        jnp.concatenate([shift_r, shift_r]),
        jnp.concatenate([-shift_i, shift_i]),
    ])

    place_of = jnp.array([0, 2, 3, 1], jnp.int32)
    clusters = jnp.arange(BLOCKS, dtype=jnp.int32)
    to_x, to_y = place_of[(clusters // 4 - x0) % 4], place_of[(clusters // 16 - y0) % 4]
    chip_place = jnp.where(core == 0, to_y * 4 + to_x, to_x * 4 + to_y)
    pos = ((((clusters // 2) % 2) ^ core) * CHIPS + chip_place) * 2 + clusters % 2
    near = near_tiles.reshape(2 * NEAR, BS, BS)
    colf = column_factor_tiles.reshape(SLOTS_HERE * RANK, BS)
    left_t = left_factors.reshape(SLOTS_HERE * RANK, BS).T
    whole = jnp.concatenate([near_columns.reshape(-1), tile_cols, tile_rows - me * 2, tile_counts])
    tables_own = (near, colf, left_t)
    pieces = lax.all_to_all(
        spectrum(histories[0], hi, lo).reshape(N_FREQ * N_ROWS, 16, L), ("freq", "rows"),
        split_axis=0, concat_axis=0, tiled=True)
    whole_s = to_other_core(whole)
    tables_other = tuple(to_other_core(t) for t in tables_own)
    spec, spec_s = regroup(core.reshape(1), pieces)
    every = gather_chips(spec) + gather_chips(spec_s)

    def scalars_of(w):
        return (w[:16], w[16:80], w[80:144], w[144:145], pos, vec)

    scalars, scalars_s = scalars_of(whole), scalars_of(whole_s)

    corr, res, sol, dens = operator(True, True, scalars, tables_own, every, spec)
    corr_s, res_s, sol_s = operator(True, False, scalars_s, tables_other, [dens], spec_s)
    every = gather_chips(corr) + gather_chips(corr_s)
    sol_got = to_other_core(sol_s)
    resid_s, dens = operator(False, True, scalars_s, tables_other, every, corr_s, res_s)
    resid_got = to_other_core(resid_s)
    (resid,) = operator(False, False, scalars, tables_own, [dens], corr, res)

    def assemble(mine, got):
        mine, got = mine.reshape(2, 1, HALF, 2 * BS), got.reshape(2, 1, HALF, 2 * BS)
        low, high = jnp.where(core == 0, mine, got), jnp.where(core == 0, got, mine)
        return jnp.concatenate([low, high], axis=1).reshape(2, FB, 2 * BS)

    return assemble(sol, sol_got), assemble(resid, resid_got)


def solution(mesh):
    hi, lo = tables()
    placed = (
        P(("freq", "rows"), None, None),
        P("freq"),
        P("freq"),
        P("freq", "rows", None, None, None),
        P("rows", None),
        P("freq", "rows", None, None),
        P("freq", "rows", None, None),
        P("rows"),
        P("rows"),
        P("rows"),
    )

    def run(*args):
        consts = tuple(jnp.asarray(c) for c in (hi, lo))
        return jax.shard_map(
            body,
            mesh=mesh,
            in_specs=((P(), P()),) + placed,
            out_specs=(P(None, "freq", "rows"), P(None, "freq", "rows")),
            check_vma=False,
        )(consts, *args)

    return run
```

```python
import functools
import math

import jax
import jax.numpy as jnp
import ml_dtypes
import numpy as np
from jax import lax
from jax.experimental import pallas as pl
from jax.experimental.pallas import tpu as pltpu
from jax.sharding import PartitionSpec as P

STEPS = 1024
FB = 128
BS = 512
NEAR = 8
RANK = 32
SLOTS_HERE = 64
BLOCKS = 64
N_FREQ = 4
N_ROWS = 32
SHARE = 256
W = 2 * FB
HALF = FB // 2
L = 2 * HALF
CHIPS = 16
EARLY = 56
GROUP = 8
damping = 2.0
F32 = jnp.float32
BF16 = jnp.bfloat16


def tables():
    t = np.arange(STEPS, dtype=np.int64)
    f = np.arange(N_FREQ * FB, dtype=np.int64)
    ang = (t[:, None] * f[None, :] % STEPS).astype(np.float64) * (2.0 * math.pi / STEPS)
    weight = (np.exp(-damping * t / STEPS) * (2.0 / math.sqrt(STEPS)))[:, None]
    both = np.stack([np.cos(ang) * weight, -np.sin(ang) * weight], axis=1)
    both = both.reshape(STEPS, 2, N_FREQ, 2, HALF).transpose(2, 0, 3, 1, 4).reshape(N_FREQ, STEPS, W)
    both = both.astype(np.float32)
    hi = both.astype(ml_dtypes.bfloat16)
    lo = (both - hi.astype(np.float32)).astype(ml_dtypes.bfloat16)
    return hi, lo


def dot(a, b):
    return jnp.dot(a, b, preferred_element_type=F32)


def spectrum_kernel(hist_ref, hi_ref, lo_ref, out_ref, hbuf, hibuf, lobuf, hsem, hisem, losem):
    hcopy = pltpu.make_async_copy(hist_ref, hbuf, hsem)
    hcopy.start()
    copies = []
    for b in range(N_FREQ):
        pair = (pltpu.make_async_copy(hi_ref.at[b], hibuf.at[b], hisem.at[b]),
                pltpu.make_async_copy(lo_ref.at[b], lobuf.at[b], losem.at[b]))
        copies.append(pair)
        for copy in pair:
            copy.start()
    hcopy.wait()
    h = hbuf[...].T
    hh = h.astype(BF16)
    hl = (h - hh.astype(F32)).astype(BF16)
    for b in range(N_FREQ):
        for copy in copies[b]:
            copy.wait()
        total = dot(hh, hibuf[b]) + (dot(hh, lobuf[b]) + dot(hl, hibuf[b]))
        for c in range(2):
            out_ref[b, :, c] = total[:, c * L:(c + 1) * L].astype(BF16).reshape(CHIPS, 16, L)


def spectrum(hist, hi, lo):
    return pl.pallas_call(
        spectrum_kernel,
        out_shape=jax.ShapeDtypeStruct((N_FREQ, CHIPS, 2, 16, L), BF16),
        in_specs=[pl.BlockSpec(memory_space=pl.ANY)] * 3,
        out_specs=pl.BlockSpec(memory_space=pltpu.VMEM),
        scratch_shapes=[
            pltpu.VMEM((STEPS, SHARE), F32),
            pltpu.VMEM((N_FREQ, STEPS, W), BF16),
            pltpu.VMEM((N_FREQ, STEPS, W), BF16),
            pltpu.SemaphoreType.DMA,
            pltpu.SemaphoreType.DMA((N_FREQ,)),
            pltpu.SemaphoreType.DMA((N_FREQ,)),
        ],
        compiler_params=pltpu.CompilerParams(vmem_limit_bytes=60 << 20),
        cost_estimate=pl.CostEstimate(flops=3_000_000_000, bytes_accessed=6 << 20, transcendentals=0),
        name="spectrum",
    )(hist, hi, lo)


def regroup_kernel(where, in_ref, p_ref, q_ref, wide):
    wide[...] = in_ref[...].astype(F32)
    swapped = where[0] == 1
    for i in range(2):
        for a in range(4):
            low = wide[:, i * 4 + a, :].astype(BF16)
            high = wide[:, 8 + i * 4 + a, :].astype(BF16)
            rows = slice(i * BS + a * 128, i * BS + (a + 1) * 128)
            p_ref[rows, :] = jnp.where(swapped, high, low)
            q_ref[rows, :] = jnp.where(swapped, low, high)


def regroup(where, pieces):
    vmem = pl.BlockSpec(memory_space=pltpu.VMEM)
    return pl.pallas_call(
        regroup_kernel,
        out_shape=[jax.ShapeDtypeStruct((2 * BS, L), BF16)] * 2,
        in_specs=[pl.BlockSpec(memory_space=pltpu.SMEM), vmem],
        out_specs=[vmem] * 2,
        scratch_shapes=[pltpu.VMEM((N_FREQ * N_ROWS, 16, L), F32)],
        compiler_params=pltpu.CompilerParams(vmem_limit_bytes=8 << 20),
        cost_estimate=pl.CostEstimate(flops=0, bytes_accessed=2 << 20, transcendentals=0),
        name="regroup",
    )(where, pieces)


def turn_kernel(in_ref, out_ref):
    out_ref[...] = in_ref[...].T


def turn(left):
    rows, lanes = left.shape
    return pl.pallas_call(
        turn_kernel,
        grid=(4,),
        out_shape=jax.ShapeDtypeStruct((lanes, rows), BF16),
        in_specs=[pl.BlockSpec((rows // 4, lanes), lambda i: (i, 0))],
        out_specs=pl.BlockSpec((lanes, rows // 4), lambda i: (0, i)),
        compiler_params=pltpu.CompilerParams(vmem_limit_bytes=8 << 20),
        cost_estimate=pl.CostEstimate(flops=0, bytes_accessed=4 << 20, transcendentals=0),
        name="turn",
    )(left)


def stage_kernel(near, colf, left_t, near_out, colf_out, left_out, sem):
    copies = [pltpu.make_async_copy(near.at[t], near_out.at[t], sem.at[t]) for t in range(2 * NEAR)]
    copies.append(pltpu.make_async_copy(colf, colf_out, sem.at[2 * NEAR]))
    copies.append(pltpu.make_async_copy(left_t, left_out, sem.at[2 * NEAR + 1]))
    for copy in copies:
        copy.start()
    for copy in copies:
        copy.wait()


def stage(tables):
    return pl.pallas_call(
        stage_kernel,
        out_shape=[jax.ShapeDtypeStruct(t.shape, BF16) for t in tables],
        in_specs=[pl.BlockSpec(memory_space=pl.ANY)] * 3,
        out_specs=[pl.BlockSpec(memory_space=pltpu.VMEM)] * 3,
        scratch_shapes=[pltpu.SemaphoreType.DMA((2 * NEAR + 2,))],
        compiler_params=pltpu.CompilerParams(vmem_limit_bytes=4 << 20),
        cost_estimate=pl.CostEstimate(flops=0, bytes_accessed=13 << 20, transcendentals=0),
        name="stage",
    )(*tables)


def join_kernel(a, b, c, d, out, sem):
    copies = [pltpu.make_async_copy(ref, out.at[k], sem.at[k]) for k, ref in enumerate((a, b, c, d))]
    for copy in copies:
        copy.start()
    for copy in copies:
        copy.wait()


def join(parts):
    rows, lanes = parts[0].shape
    return pl.pallas_call(
        join_kernel,
        out_shape=jax.ShapeDtypeStruct((4, rows, lanes), BF16),
        in_specs=[pl.BlockSpec(memory_space=pl.ANY)] * 4,
        out_specs=pl.BlockSpec(memory_space=pltpu.VMEM),
        scratch_shapes=[pltpu.SemaphoreType.DMA((4,))],
        compiler_params=pltpu.CompilerParams(vmem_limit_bytes=4 << 20),
        cost_estimate=pl.CostEstimate(flops=0, bytes_accessed=2 << 20, transcendentals=0),
        name="join",
    )(*parts).reshape(4 * rows, lanes)


def add_near(acc, ncol, near, panels):
    def near_step(g, carry):
        i = lax.div(g, 2)
        total = acc[i]
        for u in range(4):
            t = g * 4 + u
            total += dot(near[t], panels(ncol[t]))
        acc[i] = total
        return carry

    lax.fori_loop(0, 2 * NEAR // 4, near_step, 0)


def add_slots(low, coef, tcol, trow, count, colf, left_t, panels, wanted):
    def slot_step(g, carry):
        base = pl.multiple_of(g * (GROUP * RANK), GROUP * RANK)
        for u in range(GROUP):
            j = g * GROUP + u
            rows = pl.ds(pl.multiple_of(base + u * RANK, RANK), RANK)
            val = dot(colf[rows, :], panels(tcol[j]))
            used = (j < count) & wanted(tcol[j])
            for i in range(2):
                mask = jnp.where(used & (trow[j] == i), 1.0, 0.0).astype(F32)
                coef[u * RANK:(u + 1) * RANK, i * L:(i + 1) * L] = (val * mask).astype(BF16)
        low[...] += dot(left_t[:, pl.ds(base, GROUP * RANK)], coef[...])
        return carry

    lax.fori_loop(0, lax.div(count + GROUP - 1, GROUP), slot_step, 0)


def finish(first, vec, total, extra, outs):
    def swap(x):
        return pltpu.roll(x, HALF, 1)

    by_a, by_b, s_c, s_d = vec[0:1, :], vec[1:2, :], vec[2:3, :], vec[3:4, :]
    for i in range(2):
        rows = slice(i * BS, (i + 1) * BS)
        k = total(i)
        if first:
            corr_out, res_out, sol_out = outs
            x = extra[0][rows, :].astype(F32)
            f = (x * by_a + swap(x) * by_b).astype(BF16).astype(F32)
            res = x - (f * s_c + swap(f) * s_d) - (k * by_a + swap(k) * by_b)
            corr = (res * by_a + swap(res) * by_b).astype(BF16)
            corr_out[rows, :] = corr
            res_out[rows, :] = res
            sol_out[:, rows] = (f + corr.astype(F32)).T
        else:
            corr_in, res_in = extra
            c = corr_in[rows, :].astype(F32)
            outs[0][:, rows] = (res_in[rows, :] - (c * s_c + swap(c) * s_d) - k).T


def early_kernel(ncol, tcol, trow, cnt, pos, near, colf, left_t, *rest):
    dens, (acc, low, vm, coef, gsem) = rest[:8], rest[8:]
    copies, at = [], 0
    for k, d in enumerate(dens):
        size = d.shape[0]
        copies.append(pltpu.make_async_copy(d, vm.at[pl.ds(at, size)], gsem.at[k]))
        at += size
    for copy in copies:
        copy.start()
    acc[...] = jnp.zeros_like(acc)
    low[...] = jnp.zeros_like(low)
    for copy in copies:
        copy.wait()

    def panels(c):
        x = vm[jnp.minimum(pos[c], EARLY - 1)]
        return jnp.where(pos[c] < EARLY, x, jnp.zeros_like(x))

    add_near(acc, ncol, near, panels)
    add_slots(low, coef, tcol, trow, cnt[0], colf, left_t, panels, lambda c: pos[c] < EARLY)


def late_kernel(first, ncol, tcol, trow, cnt, pos, vec, near, colf, left_t, lo, hi, acc_in, low_in, *rest):
    extra, rest = (rest[:1], rest[1:]) if first else (rest[:2], rest[2:])
    outs, rest = (rest[:3], rest[3:]) if first else (rest[:1], rest[1:])
    vm, acc, low, coef, gsem = rest
    copies = [pltpu.make_async_copy(d, vm.at[pl.ds(4 * k, 4)], gsem.at[k]) for k, d in enumerate((lo, hi))]
    for copy in copies:
        copy.start()
    acc[...] = acc_in[...]
    low[...] = low_in[...]
    for copy in copies:
        copy.wait()

    def near_step(t, carry):
        place = pos[ncol[t]]

        @pl.when(place >= EARLY)
        def _():
            acc[lax.div(t, NEAR)] += dot(near[t], vm[jnp.maximum(place - EARLY, 0)])

        return carry

    lax.fori_loop(0, 2 * NEAR, near_step, 0)

    def slot_step(j, carry):
        place = pos[tcol[j]]

        @pl.when(place >= EARLY)
        def _():
            g = lax.div(j, GROUP)
            base = pl.multiple_of(g * (GROUP * RANK), GROUP * RANK)
            at = pl.multiple_of((j - g * GROUP) * RANK, RANK)
            val = dot(colf[pl.ds(pl.multiple_of(j * RANK, RANK), RANK), :], vm[jnp.maximum(place - EARLY, 0)])
            coef[...] = jnp.zeros_like(coef)
            for i in range(2):
                mask = jnp.where(trow[j] == i, 1.0, 0.0).astype(F32)
                coef[pl.ds(at, RANK), i * L:(i + 1) * L] = (val * mask).astype(BF16)
            low[...] += dot(left_t[:, pl.ds(base, GROUP * RANK)], coef[...])

        return carry

    lax.fori_loop(0, cnt[0], slot_step, 0)
    finish(first, vec, lambda i: acc[i] + low[:, i * L:(i + 1) * L], extra, outs)


def full_kernel(first, n_dens, ncol, tcol, trow, cnt, pos, vec, near, colf, left_t, *rest):
    dens, rest = rest[:n_dens], rest[n_dens:]
    extra, rest = (rest[:1], rest[1:]) if first else (rest[:2], rest[2:])
    outs, rest = (rest[:3], rest[3:]) if first else (rest[:1], rest[1:])
    copies = []
    if n_dens > 2:
        vm, acc, low, coef, gsem = rest
        at = 0
        for k, d in enumerate(dens):
            size = d.shape[0]
            copies.append(pltpu.make_async_copy(d, vm.at[pl.ds(at, size)], gsem.at[k]))
            copies[-1].start()
            at += size
    else:
        acc, low, coef = rest
        vm, late = dens[0], dens[-1]
    acc[...] = jnp.zeros_like(acc)
    low[...] = jnp.zeros_like(low)
    for copy in copies:
        copy.wait()

    def panels(c):
        place = pos[c]
        if n_dens != 2:
            return vm[place]
        return jnp.where(place < EARLY, vm[jnp.minimum(place, EARLY - 1)], late[jnp.maximum(place - EARLY, 0)])

    add_near(acc, ncol, near, panels)
    add_slots(low, coef, tcol, trow, cnt[0], colf, left_t, panels, lambda c: c >= 0)
    finish(first, vec, lambda i: acc[i] + low[:, i * L:(i + 1) * L], extra, outs)


SMEM_SPEC = pl.BlockSpec(memory_space=pltpu.SMEM)
VMEM_SPEC = pl.BlockSpec(memory_space=pltpu.VMEM)
ANY_SPEC = pl.BlockSpec(memory_space=pl.ANY)
ACC = jax.ShapeDtypeStruct((2, BS, L), F32)
LOW = jax.ShapeDtypeStruct((BS, 2 * L), F32)
COEF = jax.ShapeDtypeStruct((GROUP * RANK, 2 * L), BF16)
PLACES = jax.ShapeDtypeStruct((EARLY, BS, L), BF16)
ALL_PLACES = jax.ShapeDtypeStruct((4 * CHIPS, BS, L), BF16)
LATE = jax.ShapeDtypeStruct((4 * CHIPS - EARLY, BS, L), BF16)
TURNED = jax.ShapeDtypeStruct((L, 2 * BS), F32)
FIRST_OUTS = [jax.ShapeDtypeStruct((2 * BS, L), BF16), jax.ShapeDtypeStruct((2 * BS, L), F32), TURNED]


def scratch(*shapes):
    return [pltpu.VMEM(x.shape, x.dtype) for x in shapes]


def operator_call(kernel, name, flops, in_specs, outs, scratch_shapes, args):
    return pl.pallas_call(
        kernel,
        out_shape=outs,
        in_specs=in_specs,
        out_specs=[VMEM_SPEC] * len(outs),
        scratch_shapes=scratch_shapes,
        compiler_params=pltpu.CompilerParams(vmem_limit_bytes=8 << 20),
        cost_estimate=pl.CostEstimate(flops=flops, bytes_accessed=21 << 20, transcendentals=0),
        name=name,
    )(*args)


def operator_split(first, scalars, vec, tables, every, *extra):
    every = [d.reshape(-1, BS, L) for d in every]
    acc, low, places = operator_call(
        early_kernel, "operator_early", 6_000_000_000,
        [SMEM_SPEC] * 5 + [VMEM_SPEC] * 3 + [ANY_SPEC] * 8, [ACC, LOW, PLACES],
        scratch(COEF) + [pltpu.SemaphoreType.DMA((8,))], (*scalars, *tables, *every[:8]))
    *outs, late = operator_call(
        functools.partial(late_kernel, first), "operator_late", 1_000_000_000,
        [SMEM_SPEC] * 5 + [VMEM_SPEC] * 4 + [ANY_SPEC] * 2 + [VMEM_SPEC] * (2 + len(extra)),
        (FIRST_OUTS if first else [TURNED]) + [LATE],
        scratch(ACC, LOW, COEF) + [pltpu.SemaphoreType.DMA((2,))],
        (*scalars, vec, *tables, *every[8:], acc, low, *extra))
    return outs, (places, late)


def operator_full(first, scalars, vec, tables, dens, *extra):
    load = len(dens) > 2
    outs = FIRST_OUTS if first else [TURNED]
    dens = [d.reshape(-1, BS, L) for d in dens]
    return operator_call(
        functools.partial(full_kernel, first, len(dens)), "operator_full", 6_000_000_000,
        [SMEM_SPEC] * 5 + [VMEM_SPEC] * 4 + [ANY_SPEC if load else VMEM_SPEC] * len(dens) + [VMEM_SPEC] * len(extra),
        outs + [ALL_PLACES] if load else outs,
        scratch(ACC, LOW, COEF) + ([pltpu.SemaphoreType.DMA((len(dens),))] if load else []),
        (*scalars, vec, *tables, *dens, *extra))


def index_of(y, x, core):
    return ((y % 4) * 4 + x % 4) * 2 + core


def step_pairs(stage, shift):
    pairs = []
    for y in range(4):
        for x in range(4):
            for core in range(2):
                along_x = (stage == 0) == (core == 0)
                target = index_of(y, x + shift, core) if along_x else index_of(y + shift, x, core)
                pairs.append((index_of(y, x, core), target))
    return pairs


def shifted(v, stage, shift):
    return lax.ppermute(v, "rows", step_pairs(stage, shift))


def to_other_core(v):
    return lax.ppermute(v, "rows", [(i, i ^ 1) for i in range(N_ROWS)])


def first_step(v):
    return [v, shifted(v, 0, 1), shifted(v, 0, -1), shifted(v, 0, 2)]


def second_step(parts):
    n = parts[0].shape[0]
    line = join(parts)
    line_before, line_after = shifted(line, 1, 1), shifted(line, 1, -1)
    across_lo = shifted(line_before[:2 * n], 1, 1)
    across_hi = shifted(line_after[2 * n:], 1, -1)
    return [line, line_before, line_after, across_lo, across_hi]


def body(consts, histories, shift_real, shift_imag, near_tiles, near_columns, left_factors,
         column_factor_tiles, tile_rows, tile_cols, tile_counts):
    hi, lo = consts
    me = lax.axis_index("rows")
    core, x0, y0 = me % 2, (me // 2) % 4, me // 8

    def own_half(s):
        return jnp.where(core == 0, s[:HALF], s[HALF:])

    shift_r, shift_i = own_half(shift_real), own_half(shift_imag)
    modulus = shift_r * shift_r + shift_i * shift_i
    inv_r, inv_i = shift_r / modulus, shift_i / modulus
    vec = jnp.stack([
        jnp.concatenate([inv_r, inv_r]),
        jnp.concatenate([inv_i, -inv_i]),
        jnp.concatenate([shift_r, shift_r]),
        jnp.concatenate([-shift_i, shift_i]),
    ])

    place_of = jnp.array([0, 2, 3, 1], jnp.int32)
    clusters = jnp.arange(BLOCKS, dtype=jnp.int32)
    to_x, to_y = place_of[(clusters // 4 - x0) % 4], place_of[(clusters // 16 - y0) % 4]
    chip_place = jnp.where(core == 0, to_y * 4 + to_x, to_x * 4 + to_y)
    pos = ((((clusters // 2) % 2) ^ core) * CHIPS + chip_place) * 2 + clusters % 2
    near = near_tiles.reshape(2 * NEAR, BS, BS)
    colf = column_factor_tiles.reshape(SLOTS_HERE * RANK, BS)
    left = left_factors.reshape(SLOTS_HERE * RANK, BS)
    whole = jnp.concatenate([near_columns.reshape(-1), tile_cols, tile_rows - me * 2, tile_counts])
    spectra, left_late = lax.optimization_barrier((spectrum(histories[0], hi, lo), left))
    left_t = turn(left_late)
    pieces = lax.all_to_all(
        spectra.reshape(N_FREQ * N_ROWS, 16, L), ("freq", "rows"), split_axis=0, concat_axis=0, tiled=True)
    whole_s = to_other_core(whole)
    near_s, colf_s, left_s = to_other_core(near), to_other_core(colf), to_other_core(left)
    tables_other = (near_s, colf_s, turn(left_s))
    pieces, whole_s, tables_other, left_t = lax.optimization_barrier((pieces, whole_s, tables_other, left_t))
    tables_own = (near, colf, left_t)
    spec, spec_s = regroup(core.reshape(1), pieces)
    every = second_step(first_step(spec)) + second_step(first_step(spec_s))

    def scalars_of(w):
        return (w[:16], w[16:80], w[80:144], w[144:145], pos)

    scalars, scalars_s = scalars_of(whole), scalars_of(whole_s)

    corr, res, sol, dens = operator_full(True, scalars, vec, tables_own, every, spec)
    corr, *tables_other = lax.optimization_barrier((corr, *tables_other))
    tables_other = stage(tables_other)
    corr_s, res_s, sol_s = operator_full(True, scalars_s, vec, tables_other, [dens], spec_s)
    every = second_step(first_step(corr)) + second_step(first_step(corr_s))
    sol_got = to_other_core(sol_s)
    (resid_s,), dens = operator_split(False, scalars_s, vec, tables_other, every, corr_s, res_s)
    resid_got = to_other_core(resid_s)
    (resid,) = operator_full(False, scalars, vec, tables_own, dens, corr, res)

    def assemble(mine, got):
        mine, got = mine.reshape(2, 1, HALF, 2 * BS), got.reshape(2, 1, HALF, 2 * BS)
        low, high = jnp.where(core == 0, mine, got), jnp.where(core == 0, got, mine)
        return jnp.concatenate([low, high], axis=1).reshape(2, FB, 2 * BS)

    return assemble(sol, sol_got), assemble(resid, resid_got)


def solution(mesh):
    hi, lo = tables()
    placed = (
        P(("freq", "rows"), None, None),
        P("freq"),
        P("freq"),
        P("freq", "rows", None, None, None),
        P("rows", None),
        P("freq", "rows", None, None),
        P("freq", "rows", None, None),
        P("rows"),
        P("rows"),
        P("rows"),
    )

    def run(*args):
        consts = tuple(jnp.asarray(c) for c in (hi, lo))
        return jax.shard_map(
            body,
            mesh=mesh,
            in_specs=((P(), P()),) + placed,
            out_specs=(P(None, "freq", "rows"), P(None, "freq", "rows")),
            check_vma=False,
        )(consts, *args)

    return run
```

```python
import functools
import math

import jax
import jax.numpy as jnp
import ml_dtypes
import numpy as np
from jax import lax
from jax.experimental import pallas as pl
from jax.experimental.pallas import tpu as pltpu
from jax.sharding import PartitionSpec as P

STEPS = 1024
FB = 128
BS = 512
NEAR = 8
RANK = 32
SLOTS_HERE = 64
BLOCKS = 64
N_FREQ = 4
N_ROWS = 32
SHARE = 256
W = 2 * FB
HALF = FB // 2
L = 2 * HALF
CHIPS = 16
EARLY = 56
GROUP = 8
damping = 2.0
F32 = jnp.float32
BF16 = jnp.bfloat16


def tables():
    t = np.arange(STEPS, dtype=np.int64)
    f = np.arange(N_FREQ * FB, dtype=np.int64)
    ang = (t[:, None] * f[None, :] % STEPS).astype(np.float64) * (2.0 * math.pi / STEPS)
    weight = (np.exp(-damping * t / STEPS) * (2.0 / math.sqrt(STEPS)))[:, None]
    both = np.stack([np.cos(ang) * weight, -np.sin(ang) * weight], axis=1)
    both = both.reshape(STEPS, 2, N_FREQ, 2, HALF).transpose(2, 0, 3, 1, 4).reshape(N_FREQ, STEPS, W)
    both = both.astype(np.float32)
    hi = both.astype(ml_dtypes.bfloat16)
    lo = (both - hi.astype(np.float32)).astype(ml_dtypes.bfloat16)
    return hi, lo


def dot(a, b):
    return jnp.dot(a, b, preferred_element_type=F32)


def spectrum_kernel(hist_ref, hi_ref, lo_ref, out_ref, hbuf, hibuf, lobuf, hsem, hisem, losem):
    hcopy = pltpu.make_async_copy(hist_ref, hbuf, hsem)
    hcopy.start()
    copies = []
    for b in range(N_FREQ):
        pair = (pltpu.make_async_copy(hi_ref.at[b], hibuf.at[b], hisem.at[b]),
                pltpu.make_async_copy(lo_ref.at[b], lobuf.at[b], losem.at[b]))
        copies.append(pair)
        for copy in pair:
            copy.start()
    hcopy.wait()
    h = hbuf[...].T
    hh = h.astype(BF16)
    hl = (h - hh.astype(F32)).astype(BF16)
    for b in range(N_FREQ):
        for copy in copies[b]:
            copy.wait()
        total = dot(hh, hibuf[b]) + (dot(hh, lobuf[b]) + dot(hl, hibuf[b]))
        for c in range(2):
            out_ref[b, :, c] = total[:, c * L:(c + 1) * L].astype(BF16).reshape(CHIPS, 16, L)


def spectrum(hist, hi, lo):
    return pl.pallas_call(
        spectrum_kernel,
        out_shape=jax.ShapeDtypeStruct((N_FREQ, CHIPS, 2, 16, L), BF16),
        in_specs=[pl.BlockSpec(memory_space=pl.ANY)] * 3,
        out_specs=pl.BlockSpec(memory_space=pltpu.VMEM),
        scratch_shapes=[
            pltpu.VMEM((STEPS, SHARE), F32),
            pltpu.VMEM((N_FREQ, STEPS, W), BF16),
            pltpu.VMEM((N_FREQ, STEPS, W), BF16),
            pltpu.SemaphoreType.DMA,
            pltpu.SemaphoreType.DMA((N_FREQ,)),
            pltpu.SemaphoreType.DMA((N_FREQ,)),
        ],
        compiler_params=pltpu.CompilerParams(vmem_limit_bytes=60 << 20),
        cost_estimate=pl.CostEstimate(flops=3_000_000_000, bytes_accessed=6 << 20, transcendentals=0),
        name="spectrum",
    )(hist, hi, lo)


def regroup_kernel(where, in_ref, p_ref, q_ref, wide):
    wide[...] = in_ref[...].astype(F32)
    swapped = where[0] == 1
    for i in range(2):
        for a in range(4):
            low = wide[:, i * 4 + a, :].astype(BF16)
            high = wide[:, 8 + i * 4 + a, :].astype(BF16)
            rows = slice(i * BS + a * 128, i * BS + (a + 1) * 128)
            p_ref[rows, :] = jnp.where(swapped, high, low)
            q_ref[rows, :] = jnp.where(swapped, low, high)


def regroup(where, pieces):
    vmem = pl.BlockSpec(memory_space=pltpu.VMEM)
    return pl.pallas_call(
        regroup_kernel,
        out_shape=[jax.ShapeDtypeStruct((2 * BS, L), BF16)] * 2,
        in_specs=[pl.BlockSpec(memory_space=pltpu.SMEM), vmem],
        out_specs=[vmem] * 2,
        scratch_shapes=[pltpu.VMEM((N_FREQ * N_ROWS, 16, L), F32)],
        compiler_params=pltpu.CompilerParams(vmem_limit_bytes=8 << 20),
        cost_estimate=pl.CostEstimate(flops=0, bytes_accessed=2 << 20, transcendentals=0),
        name="regroup",
    )(where, pieces)


def turn_kernel(in_ref, out_ref):
    out_ref[...] = in_ref[...].T


def turn(left):
    rows, lanes = left.shape
    return pl.pallas_call(
        turn_kernel,
        grid=(4,),
        out_shape=jax.ShapeDtypeStruct((lanes, rows), BF16),
        in_specs=[pl.BlockSpec((rows // 4, lanes), lambda i: (i, 0))],
        out_specs=pl.BlockSpec((lanes, rows // 4), lambda i: (0, i)),
        compiler_params=pltpu.CompilerParams(vmem_limit_bytes=8 << 20),
        cost_estimate=pl.CostEstimate(flops=0, bytes_accessed=4 << 20, transcendentals=0),
        name="turn",
    )(left)


def stage_kernel(near, colf, left_t, *rest):
    near_out, (colf_out, left_out, sem) = rest[:4], rest[4:]
    copies = [pltpu.make_async_copy(near.at[t], near_out[t // 4].at[t % 4], sem.at[t]) for t in range(2 * NEAR)]
    copies.append(pltpu.make_async_copy(colf, colf_out, sem.at[2 * NEAR]))
    copies.append(pltpu.make_async_copy(left_t, left_out, sem.at[2 * NEAR + 1]))
    for copy in copies:
        copy.start()
    for copy in copies:
        copy.wait()


def stage(tables):
    return pl.pallas_call(
        stage_kernel,
        out_shape=[jax.ShapeDtypeStruct((4, BS, BS), BF16)] * 4 + [jax.ShapeDtypeStruct(t.shape, BF16) for t in tables[1:]],
        in_specs=[pl.BlockSpec(memory_space=pl.ANY)] * 3,
        out_specs=[pl.BlockSpec(memory_space=pltpu.VMEM)] * 6,
        scratch_shapes=[pltpu.SemaphoreType.DMA((2 * NEAR + 2,))],
        compiler_params=pltpu.CompilerParams(vmem_limit_bytes=4 << 20),
        cost_estimate=pl.CostEstimate(flops=0, bytes_accessed=13 << 20, transcendentals=0),
        name="stage",
    )(*tables)


def join_kernel(a, b, c, d, out, sem):
    copies = [pltpu.make_async_copy(ref, out.at[k], sem.at[k]) for k, ref in enumerate((a, b, c, d))]
    for copy in copies:
        copy.start()
    for copy in copies:
        copy.wait()


def join(parts):
    rows, lanes = parts[0].shape
    return pl.pallas_call(
        join_kernel,
        out_shape=jax.ShapeDtypeStruct((4, rows, lanes), BF16),
        in_specs=[pl.BlockSpec(memory_space=pl.ANY)] * 4,
        out_specs=pl.BlockSpec(memory_space=pltpu.VMEM),
        scratch_shapes=[pltpu.SemaphoreType.DMA((4,))],
        compiler_params=pltpu.CompilerParams(vmem_limit_bytes=4 << 20),
        cost_estimate=pl.CostEstimate(flops=0, bytes_accessed=2 << 20, transcendentals=0),
        name="join",
    )(*parts).reshape(4 * rows, lanes)


def add_near(acc, ncol, near, panels):
    for g in range(4):
        total = acc[g // 2]
        for u in range(4):
            total += dot(near[g][u], panels(ncol[g * 4 + u]))
        acc[g // 2] = total


def add_slots(low, coef, tcol, trow, count, colf, left_t, panels, wanted):
    def slot_step(g, carry):
        base = pl.multiple_of(g * (GROUP * RANK), GROUP * RANK)
        for u in range(GROUP):
            j = g * GROUP + u
            rows = pl.ds(pl.multiple_of(base + u * RANK, RANK), RANK)
            val = dot(colf[rows, :], panels(tcol[j]))
            used = (j < count) & wanted(tcol[j])
            for i in range(2):
                mask = jnp.where(used & (trow[j] == i), 1.0, 0.0).astype(F32)
                coef[u * RANK:(u + 1) * RANK, i * L:(i + 1) * L] = (val * mask).astype(BF16)
        low[...] += dot(left_t[:, pl.ds(base, GROUP * RANK)], coef[...])
        return carry

    lax.fori_loop(0, lax.div(count + GROUP - 1, GROUP), slot_step, 0)


def finish(first, vec, total, extra, outs):
    def swap(x):
        return pltpu.roll(x, HALF, 1)

    by_a, by_b, s_c, s_d = vec[0:1, :], vec[1:2, :], vec[2:3, :], vec[3:4, :]
    for i in range(2):
        rows = slice(i * BS, (i + 1) * BS)
        k = total(i)
        if first:
            corr_out, res_out, sol_out = outs
            x = extra[0][rows, :].astype(F32)
            f = (x * by_a + swap(x) * by_b).astype(BF16).astype(F32)
            res = x - (f * s_c + swap(f) * s_d) - (k * by_a + swap(k) * by_b)
            corr = (res * by_a + swap(res) * by_b).astype(BF16)
            corr_out[rows, :] = corr
            res_out[rows, :] = res
            sol_out[:, rows] = (f + corr.astype(F32)).T
        else:
            corr_in, res_in = extra
            c = corr_in[rows, :].astype(F32)
            outs[0][:, rows] = (res_in[rows, :] - (c * s_c + swap(c) * s_d) - k).T


def early_kernel(ncol, tcol, trow, cnt, pos, *rest):
    near, (colf, left_t), rest = rest[:4], rest[4:6], rest[6:]
    dens, (acc, low, vm, coef, gsem) = rest[:8], rest[8:]
    copies, at = [], 0
    for k, d in enumerate(dens):
        size = d.shape[0]
        copies.append(pltpu.make_async_copy(d, vm.at[pl.ds(at, size)], gsem.at[k]))
        at += size
    for copy in copies:
        copy.start()
    acc[...] = jnp.zeros_like(acc)
    low[...] = jnp.zeros_like(low)
    for copy in copies:
        copy.wait()

    def panels(c):
        x = vm[jnp.minimum(pos[c], EARLY - 1)]
        return jnp.where(pos[c] < EARLY, x, jnp.zeros_like(x))

    add_near(acc, ncol, near, panels)
    add_slots(low, coef, tcol, trow, cnt[0], colf, left_t, panels, lambda c: pos[c] < EARLY)


def late_kernel(first, ncol, tcol, trow, cnt, pos, vec, *rest):
    near, (colf, left_t, lo, hi, acc_in, low_in), rest = rest[:4], rest[4:10], rest[10:]
    extra, rest = (rest[:1], rest[1:]) if first else (rest[:2], rest[2:])
    outs, rest = (rest[:3], rest[3:]) if first else (rest[:1], rest[1:])
    vm, acc, low, coef, gsem = rest
    copies = [pltpu.make_async_copy(d, vm.at[pl.ds(4 * k, 4)], gsem.at[k]) for k, d in enumerate((lo, hi))]
    for copy in copies:
        copy.start()
    acc[...] = acc_in[...]
    low[...] = low_in[...]
    for copy in copies:
        copy.wait()

    for g in range(4):
        def near_step(u, carry, g=g):
            place = pos[ncol[g * 4 + u]]

            @pl.when(place >= EARLY)
            def _():
                acc[g // 2] += dot(near[g][u], vm[jnp.maximum(place - EARLY, 0)])

            return carry

        lax.fori_loop(0, 4, near_step, 0)

    def slot_step(j, carry):
        place = pos[tcol[j]]

        @pl.when(place >= EARLY)
        def _():
            g = lax.div(j, GROUP)
            base = pl.multiple_of(g * (GROUP * RANK), GROUP * RANK)
            at = pl.multiple_of((j - g * GROUP) * RANK, RANK)
            val = dot(colf[pl.ds(pl.multiple_of(j * RANK, RANK), RANK), :], vm[jnp.maximum(place - EARLY, 0)])
            coef[...] = jnp.zeros_like(coef)
            for i in range(2):
                mask = jnp.where(trow[j] == i, 1.0, 0.0).astype(F32)
                coef[pl.ds(at, RANK), i * L:(i + 1) * L] = (val * mask).astype(BF16)
            low[...] += dot(left_t[:, pl.ds(base, GROUP * RANK)], coef[...])

        return carry

    lax.fori_loop(0, cnt[0], slot_step, 0)
    finish(first, vec, lambda i: acc[i] + low[:, i * L:(i + 1) * L], extra, outs)


def full_kernel(first, n_dens, ncol, tcol, trow, cnt, pos, vec, *rest):
    near, (colf, left_t), rest = rest[:4], rest[4:6], rest[6:]
    dens, rest = rest[:n_dens], rest[n_dens:]
    extra, rest = (rest[:1], rest[1:]) if first else (rest[:2], rest[2:])
    outs, rest = (rest[:3], rest[3:]) if first else (rest[:1], rest[1:])
    copies = []
    if n_dens > 2:
        vm, late, acc, low, coef, gsem = rest
        at = 0
        for k, d in enumerate(dens):
            size = d.shape[0]
            place, start = (vm, at) if at < 2 * CHIPS else (late, at - 2 * CHIPS)
            copies.append(pltpu.make_async_copy(d, place.at[pl.ds(start, size)], gsem.at[k]))
            copies[-1].start()
            at += size
    else:
        acc, low, coef = rest
        vm, late = dens[0], dens[-1]
    acc[...] = jnp.zeros_like(acc)
    low[...] = jnp.zeros_like(low)
    for copy in copies:
        copy.wait()

    def panels(c):
        place = pos[c]
        split = vm.shape[0]
        return jnp.where(place < split, vm[jnp.minimum(place, split - 1)], late[jnp.maximum(place - split, 0)])

    add_near(acc, ncol, near, panels)
    add_slots(low, coef, tcol, trow, cnt[0], colf, left_t, panels, lambda c: c >= 0)
    finish(first, vec, lambda i: acc[i] + low[:, i * L:(i + 1) * L], extra, outs)


SMEM_SPEC = pl.BlockSpec(memory_space=pltpu.SMEM)
VMEM_SPEC = pl.BlockSpec(memory_space=pltpu.VMEM)
ANY_SPEC = pl.BlockSpec(memory_space=pl.ANY)
ACC = jax.ShapeDtypeStruct((2, BS, L), F32)
LOW = jax.ShapeDtypeStruct((BS, 2 * L), F32)
COEF = jax.ShapeDtypeStruct((GROUP * RANK, 2 * L), BF16)
PLACES = jax.ShapeDtypeStruct((EARLY, BS, L), BF16)
HALF_PLACES = jax.ShapeDtypeStruct((2 * CHIPS, BS, L), BF16)
LATE = jax.ShapeDtypeStruct((4 * CHIPS - EARLY, BS, L), BF16)
TURNED = jax.ShapeDtypeStruct((L, 2 * BS), F32)
FIRST_OUTS = [jax.ShapeDtypeStruct((2 * BS, L), BF16), jax.ShapeDtypeStruct((2 * BS, L), F32), TURNED]


def scratch(*shapes):
    return [pltpu.VMEM(x.shape, x.dtype) for x in shapes]


def operator_call(kernel, name, flops, in_specs, outs, scratch_shapes, args):
    return pl.pallas_call(
        kernel,
        out_shape=outs,
        in_specs=in_specs,
        out_specs=[VMEM_SPEC] * len(outs),
        scratch_shapes=scratch_shapes,
        compiler_params=pltpu.CompilerParams(vmem_limit_bytes=8 << 20),
        cost_estimate=pl.CostEstimate(flops=flops, bytes_accessed=21 << 20, transcendentals=0),
        name=name,
    )(*args)


def operator_split(first, scalars, vec, tables, every, *extra):
    every = [d.reshape(-1, BS, L) for d in every]
    acc, low, places = operator_call(
        early_kernel, "operator_early", 6_000_000_000,
        [SMEM_SPEC] * 5 + [VMEM_SPEC] * 6 + [ANY_SPEC] * 8, [ACC, LOW, PLACES],
        scratch(COEF) + [pltpu.SemaphoreType.DMA((8,))], (*scalars, *tables, *every[:8]))
    *outs, late = operator_call(
        functools.partial(late_kernel, first), "operator_late", 1_000_000_000,
        [SMEM_SPEC] * 5 + [VMEM_SPEC] * 7 + [ANY_SPEC] * 2 + [VMEM_SPEC] * (2 + len(extra)),
        (FIRST_OUTS if first else [TURNED]) + [LATE],
        scratch(ACC, LOW, COEF) + [pltpu.SemaphoreType.DMA((2,))],
        (*scalars, vec, *tables, *every[8:], acc, low, *extra))
    return outs, (places, late)


def operator_full(first, scalars, vec, tables, dens, *extra):
    load = len(dens) > 2
    outs = FIRST_OUTS if first else [TURNED]
    dens = [d.reshape(-1, BS, L) for d in dens]
    return operator_call(
        functools.partial(full_kernel, first, len(dens)), "operator_full", 6_000_000_000,
        [SMEM_SPEC] * 5 + [VMEM_SPEC] * 7 + [ANY_SPEC if load else VMEM_SPEC] * len(dens) + [VMEM_SPEC] * len(extra),
        outs + [HALF_PLACES] * 2 if load else outs,
        scratch(ACC, LOW, COEF) + ([pltpu.SemaphoreType.DMA((len(dens),))] if load else []),
        (*scalars, vec, *tables, *dens, *extra))


def assemble_kernel(which, mine, got, out, sem):
    copies = []
    for k, ref in enumerate((mine, got)):
        half = which[0] if k == 0 else 1 - which[0]
        for part in range(2):
            copies.append(pltpu.make_async_copy(
                ref.at[part], out.at[part, pl.ds(pl.multiple_of(half * HALF, HALF), HALF)], sem.at[2 * k + part]))
    for copy in copies:
        copy.start()
    for copy in copies:
        copy.wait()


def assemble(which, mine, got):
    return pl.pallas_call(
        assemble_kernel,
        out_shape=jax.ShapeDtypeStruct((2, FB, 2 * BS), F32),
        in_specs=[SMEM_SPEC, VMEM_SPEC, VMEM_SPEC],
        out_specs=ANY_SPEC,
        scratch_shapes=[pltpu.SemaphoreType.DMA((4,))],
        compiler_params=pltpu.CompilerParams(vmem_limit_bytes=4 << 20),
        cost_estimate=pl.CostEstimate(flops=0, bytes_accessed=2 << 20, transcendentals=0),
        name="assemble",
    )(which, mine.reshape(2, HALF, 2 * BS), got.reshape(2, HALF, 2 * BS))


def index_of(y, x, core):
    return ((y % 4) * 4 + x % 4) * 2 + core


def step_pairs(stage, shift):
    pairs = []
    for y in range(4):
        for x in range(4):
            for core in range(2):
                along_x = (stage == 0) == (core == 0)
                target = index_of(y, x + shift, core) if along_x else index_of(y + shift, x, core)
                pairs.append((index_of(y, x, core), target))
    return pairs


def shifted(v, stage, shift):
    return lax.ppermute(v, "rows", step_pairs(stage, shift))


def to_other_core(v):
    return lax.ppermute(v, "rows", [(i, i ^ 1) for i in range(N_ROWS)])


def first_step(v):
    return [v, shifted(v, 0, 1), shifted(v, 0, -1), shifted(v, 0, 2)]


def second_step(parts):
    n = parts[0].shape[0]
    line = join(parts)
    line_before, line_after = shifted(line, 1, 1), shifted(line, 1, -1)
    across_lo = shifted(line_before[:2 * n], 1, 1)
    across_hi = shifted(line_after[2 * n:], 1, -1)
    return [line, line_before, line_after, across_lo, across_hi]


def body(consts, histories, shift_real, shift_imag, near_tiles, near_columns, left_factors,
         column_factor_tiles, tile_rows, tile_cols, tile_counts):
    hi, lo = consts
    me = lax.axis_index("rows")
    core, x0, y0 = me % 2, (me // 2) % 4, me // 8

    def own_half(s):
        return jnp.where(core == 0, s[:HALF], s[HALF:])

    shift_r, shift_i = own_half(shift_real), own_half(shift_imag)
    modulus = shift_r * shift_r + shift_i * shift_i
    inv_r, inv_i = shift_r / modulus, shift_i / modulus
    vec = jnp.stack([
        jnp.concatenate([inv_r, inv_r]),
        jnp.concatenate([inv_i, -inv_i]),
        jnp.concatenate([shift_r, shift_r]),
        jnp.concatenate([-shift_i, shift_i]),
    ])

    place_of = jnp.array([0, 2, 3, 1], jnp.int32)
    clusters = jnp.arange(BLOCKS, dtype=jnp.int32)
    to_x, to_y = place_of[(clusters // 4 - x0) % 4], place_of[(clusters // 16 - y0) % 4]
    chip_place = jnp.where(core == 0, to_y * 4 + to_x, to_x * 4 + to_y)
    pos = ((((clusters // 2) % 2) ^ core) * CHIPS + chip_place) * 2 + clusters % 2
    near = near_tiles.reshape(2 * NEAR, BS, BS)
    colf = column_factor_tiles.reshape(SLOTS_HERE * RANK, BS)
    left = left_factors.reshape(SLOTS_HERE * RANK, BS)
    whole = jnp.concatenate([near_columns.reshape(-1), tile_cols, tile_rows - me * 2, tile_counts])
    spectra, left_late = lax.optimization_barrier((spectrum(histories[0], hi, lo), left))
    left_t = turn(left_late)
    pieces = lax.all_to_all(
        spectra.reshape(N_FREQ * N_ROWS, 16, L), ("freq", "rows"), split_axis=0, concat_axis=0, tiled=True)
    whole_s = to_other_core(whole)
    near_s, colf_s, left_s = to_other_core(near), to_other_core(colf), to_other_core(left)
    tables_other = (near_s, colf_s, turn(left_s))
    pieces, whole_s, tables_other, left_t = lax.optimization_barrier((pieces, whole_s, tables_other, left_t))
    tables_own = (*(near[4 * g:4 * g + 4] for g in range(4)), colf, left_t)
    spec, spec_s = regroup(core.reshape(1), pieces)
    every = second_step(first_step(spec)) + second_step(first_step(spec_s))

    def scalars_of(w):
        return (w[:16], w[16:80], w[80:144], w[144:145], pos)

    scalars, scalars_s = scalars_of(whole), scalars_of(whole_s)

    corr, res, sol, *dens = operator_full(True, scalars, vec, tables_own, every, spec)
    corr, *tables_other = lax.optimization_barrier((corr, *tables_other))
    tables_other = stage(tables_other)
    corr_s, res_s, sol_s = operator_full(True, scalars_s, vec, tables_other, dens, spec_s)
    every = second_step(first_step(corr)) + second_step(first_step(corr_s))
    sol_got = to_other_core(sol_s)
    (resid_s,), dens = operator_split(False, scalars_s, vec, tables_other, every, corr_s, res_s)
    resid_got = to_other_core(resid_s)
    (resid,) = operator_full(False, scalars, vec, tables_own, dens, corr, res)

    which = core.reshape(1)
    return assemble(which, sol, sol_got), assemble(which, resid, resid_got)


def solution(mesh):
    hi, lo = tables()
    placed = (
        P(("freq", "rows"), None, None),
        P("freq"),
        P("freq"),
        P("freq", "rows", None, None, None),
        P("rows", None),
        P("freq", "rows", None, None),
        P("freq", "rows", None, None),
        P("rows"),
        P("rows"),
        P("rows"),
    )

    def run(*args):
        consts = tuple(jnp.asarray(c) for c in (hi, lo))
        return jax.shard_map(
            body,
            mesh=mesh,
            in_specs=((P(), P()),) + placed,
            out_specs=(P(None, "freq", "rows"), P(None, "freq", "rows")),
            check_vma=False,
        )(consts, *args)

    return run
```

```python
import functools
import math

import jax
import jax.numpy as jnp
import ml_dtypes
import numpy as np
from jax import lax
from jax.experimental import pallas as pl
from jax.experimental.pallas import tpu as pltpu
from jax.sharding import PartitionSpec as P

STEPS = 1024
FB = 128
BS = 512
NEAR = 8
RANK = 32
SLOTS_HERE = 64
BLOCKS = 64
N_FREQ = 4
N_ROWS = 32
SHARE = 256
W = 2 * FB
HALF = FB // 2
L = 2 * HALF
CHIPS = 16
EARLY = 56
GROUP = 8
damping = 2.0
F32 = jnp.float32
BF16 = jnp.bfloat16


def tables():
    t = np.arange(STEPS, dtype=np.int64)
    f = np.arange(N_FREQ * FB, dtype=np.int64)
    ang = (t[:, None] * f[None, :] % STEPS).astype(np.float64) * (2.0 * math.pi / STEPS)
    weight = (np.exp(-damping * t / STEPS) * (2.0 / math.sqrt(STEPS)))[:, None]
    both = np.stack([np.cos(ang) * weight, -np.sin(ang) * weight], axis=1)
    both = both.reshape(STEPS, 2, N_FREQ, 2, HALF).transpose(2, 3, 1, 4, 0).reshape(N_FREQ, W, STEPS)
    both = both.astype(np.float32)
    hi = both.astype(ml_dtypes.bfloat16)
    lo = (both - hi.astype(np.float32)).astype(ml_dtypes.bfloat16)
    return hi, lo


def dot(a, b):
    return jnp.dot(a, b, preferred_element_type=F32)


def spectrum_kernel(hist_ref, hi_ref, lo_ref, out_ref, hbuf, hibuf, lobuf, hsem, hisem, losem):
    hcopy = pltpu.make_async_copy(hist_ref, hbuf, hsem)
    hcopy.start()
    copies = []
    for b in range(N_FREQ):
        pair = (pltpu.make_async_copy(hi_ref.at[b], hibuf.at[b], hisem.at[b]),
                pltpu.make_async_copy(lo_ref.at[b], lobuf.at[b], losem.at[b]))
        copies.append(pair)
        for copy in pair:
            copy.start()
    hcopy.wait()
    h = hbuf[...]
    hh = h.astype(BF16)
    hl = (h - hh.astype(F32)).astype(BF16)
    for pair in range(2):
        for b in (2 * pair, 2 * pair + 1):
            for copy in copies[b]:
                copy.wait()
        for b in (2 * pair, 2 * pair + 1):
            total = dot(hibuf[b], hh) + (dot(lobuf[b], hh) + dot(hibuf[b], hl))
            turned = total.astype(BF16).T
            for c in range(2):
                out_ref[b, :, c] = turned[:, c * L:(c + 1) * L].reshape(CHIPS, 16, L)


def spectrum(hist, hi, lo):
    return pl.pallas_call(
        spectrum_kernel,
        out_shape=jax.ShapeDtypeStruct((N_FREQ, CHIPS, 2, 16, L), BF16),
        in_specs=[pl.BlockSpec(memory_space=pl.ANY)] * 3,
        out_specs=pl.BlockSpec(memory_space=pltpu.VMEM),
        scratch_shapes=[
            pltpu.VMEM((STEPS, SHARE), F32),
            pltpu.VMEM((N_FREQ, W, STEPS), BF16),
            pltpu.VMEM((N_FREQ, W, STEPS), BF16),
            pltpu.SemaphoreType.DMA,
            pltpu.SemaphoreType.DMA((N_FREQ,)),
            pltpu.SemaphoreType.DMA((N_FREQ,)),
        ],
        compiler_params=pltpu.CompilerParams(vmem_limit_bytes=60 << 20),
        cost_estimate=pl.CostEstimate(flops=3_000_000_000, bytes_accessed=6 << 20, transcendentals=0),
        name="spectrum",
    )(hist, hi, lo)


def regroup_kernel(where, in_ref, p_ref, q_ref, wide):
    wide[...] = in_ref[...].astype(F32)
    swapped = where[0] == 1
    for i in range(2):
        for a in range(4):
            low = wide[:, i * 4 + a, :].astype(BF16)
            high = wide[:, 8 + i * 4 + a, :].astype(BF16)
            rows = slice(i * BS + a * 128, i * BS + (a + 1) * 128)
            p_ref[rows, :] = jnp.where(swapped, high, low)
            q_ref[rows, :] = jnp.where(swapped, low, high)


def regroup(where, pieces):
    vmem = pl.BlockSpec(memory_space=pltpu.VMEM)
    return pl.pallas_call(
        regroup_kernel,
        out_shape=[jax.ShapeDtypeStruct((2 * BS, L), BF16)] * 2,
        in_specs=[pl.BlockSpec(memory_space=pltpu.SMEM), vmem],
        out_specs=[vmem] * 2,
        scratch_shapes=[pltpu.VMEM((N_FREQ * N_ROWS, 16, L), F32)],
        compiler_params=pltpu.CompilerParams(vmem_limit_bytes=8 << 20),
        cost_estimate=pl.CostEstimate(flops=0, bytes_accessed=2 << 20, transcendentals=0),
        name="regroup",
    )(where, pieces)


def turn_kernel(in_ref, out_ref):
    out_ref[...] = in_ref[...].T


def turn(left):
    rows, lanes = left.shape
    return pl.pallas_call(
        turn_kernel,
        grid=(4,),
        out_shape=jax.ShapeDtypeStruct((lanes, rows), BF16),
        in_specs=[pl.BlockSpec((rows // 4, lanes), lambda i: (i, 0))],
        out_specs=pl.BlockSpec((lanes, rows // 4), lambda i: (0, i)),
        compiler_params=pltpu.CompilerParams(vmem_limit_bytes=8 << 20),
        cost_estimate=pl.CostEstimate(flops=0, bytes_accessed=4 << 20, transcendentals=0),
        name="turn",
    )(left)


def stage_kernel(near, colf, left_t, *rest):
    near_out, (colf_out, left_out, sem) = rest[:4], rest[4:]
    copies = [pltpu.make_async_copy(near.at[t], near_out[t // 4].at[t % 4], sem.at[t]) for t in range(2 * NEAR)]
    copies.append(pltpu.make_async_copy(colf, colf_out, sem.at[2 * NEAR]))
    copies.append(pltpu.make_async_copy(left_t, left_out, sem.at[2 * NEAR + 1]))
    for copy in copies:
        copy.start()
    for copy in copies:
        copy.wait()


def stage(tables):
    return pl.pallas_call(
        stage_kernel,
        out_shape=[jax.ShapeDtypeStruct((4, BS, BS), BF16)] * 4 + [jax.ShapeDtypeStruct(t.shape, BF16) for t in tables[1:]],
        in_specs=[pl.BlockSpec(memory_space=pl.ANY)] * 3,
        out_specs=[pl.BlockSpec(memory_space=pltpu.VMEM)] * 6,
        scratch_shapes=[pltpu.SemaphoreType.DMA((2 * NEAR + 2,))],
        compiler_params=pltpu.CompilerParams(vmem_limit_bytes=4 << 20),
        cost_estimate=pl.CostEstimate(flops=0, bytes_accessed=13 << 20, transcendentals=0),
        name="stage",
    )(*tables)


def join_kernel(a, b, c, d, out, sem):
    copies = [pltpu.make_async_copy(ref, out.at[k], sem.at[k]) for k, ref in enumerate((a, b, c, d))]
    for copy in copies:
        copy.start()
    for copy in copies:
        copy.wait()


def join(parts):
    rows, lanes = parts[0].shape
    return pl.pallas_call(
        join_kernel,
        out_shape=jax.ShapeDtypeStruct((4, rows, lanes), BF16),
        in_specs=[pl.BlockSpec(memory_space=pl.ANY)] * 4,
        out_specs=pl.BlockSpec(memory_space=pltpu.VMEM),
        scratch_shapes=[pltpu.SemaphoreType.DMA((4,))],
        compiler_params=pltpu.CompilerParams(vmem_limit_bytes=4 << 20),
        cost_estimate=pl.CostEstimate(flops=0, bytes_accessed=2 << 20, transcendentals=0),
        name="join",
    )(*parts).reshape(4 * rows, lanes)


def add_near(acc, ncol, near, panels):
    for g in range(4):
        total = acc[g // 2]
        for u in range(4):
            total += dot(near[g][u], panels(ncol[g * 4 + u]))
        acc[g // 2] = total


def add_slots(low, coef, tcol, trow, count, colf, left_t, panels, wanted):
    def slot_step(g, carry):
        base = pl.multiple_of(g * (GROUP * RANK), GROUP * RANK)
        for u in range(GROUP):
            j = g * GROUP + u
            rows = pl.ds(pl.multiple_of(base + u * RANK, RANK), RANK)
            val = dot(colf[rows, :], panels(tcol[j]))
            used = (j < count) & wanted(tcol[j])
            for i in range(2):
                mask = jnp.where(used & (trow[j] == i), 1.0, 0.0).astype(F32)
                coef[u * RANK:(u + 1) * RANK, i * L:(i + 1) * L] = (val * mask).astype(BF16)
        low[...] += dot(left_t[:, pl.ds(base, GROUP * RANK)], coef[...])
        return carry

    lax.fori_loop(0, lax.div(count + GROUP - 1, GROUP), slot_step, 0)


def finish(first, vec, total, extra, outs):
    def swap(x):
        return pltpu.roll(x, HALF, 1)

    by_a, by_b, s_c, s_d = vec[0:1, :], vec[1:2, :], vec[2:3, :], vec[3:4, :]
    for i in range(2):
        rows = slice(i * BS, (i + 1) * BS)
        k = total(i)
        if first:
            corr_out, res_out, sol_out = outs
            x = extra[0][rows, :].astype(F32)
            f = (x * by_a + swap(x) * by_b).astype(BF16).astype(F32)
            res = x - (f * s_c + swap(f) * s_d) - (k * by_a + swap(k) * by_b)
            corr = (res * by_a + swap(res) * by_b).astype(BF16)
            corr_out[rows, :] = corr
            res_out[rows, :] = res
            sol_out[:, rows] = (f + corr.astype(F32)).T
        else:
            corr_in, res_in = extra
            c = corr_in[rows, :].astype(F32)
            outs[0][:, rows] = (res_in[rows, :] - (c * s_c + swap(c) * s_d) - k).T


def early_kernel(ncol, tcol, trow, cnt, pos, *rest):
    near, (colf, left_t), rest = rest[:4], rest[4:6], rest[6:]
    dens, (acc, low, vm, coef, gsem) = rest[:8], rest[8:]
    copies, at = [], 0
    for k, d in enumerate(dens):
        size = d.shape[0]
        copies.append(pltpu.make_async_copy(d, vm.at[pl.ds(at, size)], gsem.at[k]))
        at += size
    for copy in copies:
        copy.start()
    acc[...] = jnp.zeros_like(acc)
    low[...] = jnp.zeros_like(low)
    for copy in copies:
        copy.wait()

    def panels(c):
        x = vm[jnp.minimum(pos[c], EARLY - 1)]
        return jnp.where(pos[c] < EARLY, x, jnp.zeros_like(x))

    add_near(acc, ncol, near, panels)
    add_slots(low, coef, tcol, trow, cnt[0], colf, left_t, panels, lambda c: pos[c] < EARLY)


def late_kernel(first, ncol, tcol, trow, cnt, pos, vec, *rest):
    near, (colf, left_t, lo, hi, acc_in, low_in), rest = rest[:4], rest[4:10], rest[10:]
    extra, rest = (rest[:1], rest[1:]) if first else (rest[:2], rest[2:])
    outs, rest = (rest[:3], rest[3:]) if first else (rest[:1], rest[1:])
    vm, acc, low, coef, gsem = rest
    copies = [pltpu.make_async_copy(d, vm.at[pl.ds(4 * k, 4)], gsem.at[k]) for k, d in enumerate((lo, hi))]
    for copy in copies:
        copy.start()
    acc[...] = acc_in[...]
    low[...] = low_in[...]
    for copy in copies:
        copy.wait()

    for g in range(4):
        def near_step(u, carry, g=g):
            place = pos[ncol[g * 4 + u]]

            @pl.when(place >= EARLY)
            def _():
                acc[g // 2] += dot(near[g][u], vm[jnp.maximum(place - EARLY, 0)])

            return carry

        lax.fori_loop(0, 4, near_step, 0)

    def slot_step(j, carry):
        place = pos[tcol[j]]

        @pl.when(place >= EARLY)
        def _():
            g = lax.div(j, GROUP)
            base = pl.multiple_of(g * (GROUP * RANK), GROUP * RANK)
            at = pl.multiple_of((j - g * GROUP) * RANK, RANK)
            val = dot(colf[pl.ds(pl.multiple_of(j * RANK, RANK), RANK), :], vm[jnp.maximum(place - EARLY, 0)])
            coef[...] = jnp.zeros_like(coef)
            for i in range(2):
                mask = jnp.where(trow[j] == i, 1.0, 0.0).astype(F32)
                coef[pl.ds(at, RANK), i * L:(i + 1) * L] = (val * mask).astype(BF16)
            low[...] += dot(left_t[:, pl.ds(base, GROUP * RANK)], coef[...])

        return carry

    lax.fori_loop(0, cnt[0], slot_step, 0)
    finish(first, vec, lambda i: acc[i] + low[:, i * L:(i + 1) * L], extra, outs)


def full_kernel(first, n_dens, ncol, tcol, trow, cnt, pos, vec, *rest):
    near, (colf, left_t), rest = rest[:4], rest[4:6], rest[6:]
    dens, rest = rest[:n_dens], rest[n_dens:]
    extra, rest = (rest[:1], rest[1:]) if first else (rest[:2], rest[2:])
    outs, rest = (rest[:3], rest[3:]) if first else (rest[:1], rest[1:])
    copies = []
    if n_dens > 2:
        vm, late, acc, low, coef, gsem = rest
        at = 0
        for k, d in enumerate(dens):
            size = d.shape[0]
            place, start = (vm, at) if at < 2 * CHIPS else (late, at - 2 * CHIPS)
            copies.append(pltpu.make_async_copy(d, place.at[pl.ds(start, size)], gsem.at[k]))
            copies[-1].start()
            at += size
    else:
        acc, low, coef = rest
        vm, late = dens[0], dens[-1]
    acc[...] = jnp.zeros_like(acc)
    low[...] = jnp.zeros_like(low)
    for copy in copies:
        copy.wait()

    def panels(c):
        place = pos[c]
        split = vm.shape[0]
        return jnp.where(place < split, vm[jnp.minimum(place, split - 1)], late[jnp.maximum(place - split, 0)])

    add_near(acc, ncol, near, panels)
    add_slots(low, coef, tcol, trow, cnt[0], colf, left_t, panels, lambda c: c >= 0)
    finish(first, vec, lambda i: acc[i] + low[:, i * L:(i + 1) * L], extra, outs)


SMEM_SPEC = pl.BlockSpec(memory_space=pltpu.SMEM)
VMEM_SPEC = pl.BlockSpec(memory_space=pltpu.VMEM)
ANY_SPEC = pl.BlockSpec(memory_space=pl.ANY)
ACC = jax.ShapeDtypeStruct((2, BS, L), F32)
LOW = jax.ShapeDtypeStruct((BS, 2 * L), F32)
COEF = jax.ShapeDtypeStruct((GROUP * RANK, 2 * L), BF16)
PLACES = jax.ShapeDtypeStruct((EARLY, BS, L), BF16)
HALF_PLACES = jax.ShapeDtypeStruct((2 * CHIPS, BS, L), BF16)
LATE = jax.ShapeDtypeStruct((4 * CHIPS - EARLY, BS, L), BF16)
TURNED = jax.ShapeDtypeStruct((L, 2 * BS), F32)
FIRST_OUTS = [jax.ShapeDtypeStruct((2 * BS, L), BF16), jax.ShapeDtypeStruct((2 * BS, L), F32), TURNED]


def scratch(*shapes):
    return [pltpu.VMEM(x.shape, x.dtype) for x in shapes]


def operator_call(kernel, name, flops, in_specs, outs, scratch_shapes, args):
    return pl.pallas_call(
        kernel,
        out_shape=outs,
        in_specs=in_specs,
        out_specs=[VMEM_SPEC] * len(outs),
        scratch_shapes=scratch_shapes,
        compiler_params=pltpu.CompilerParams(vmem_limit_bytes=8 << 20),
        cost_estimate=pl.CostEstimate(flops=flops, bytes_accessed=21 << 20, transcendentals=0),
        name=name,
    )(*args)


def operator_split(first, scalars, vec, tables, every, *extra):
    every = [d.reshape(-1, BS, L) for d in every]
    acc, low, places = operator_call(
        early_kernel, "operator_early", 6_000_000_000,
        [SMEM_SPEC] * 5 + [VMEM_SPEC] * 6 + [ANY_SPEC] * 8, [ACC, LOW, PLACES],
        scratch(COEF) + [pltpu.SemaphoreType.DMA((8,))], (*scalars, *tables, *every[:8]))
    *outs, late = operator_call(
        functools.partial(late_kernel, first), "operator_late", 1_000_000_000,
        [SMEM_SPEC] * 5 + [VMEM_SPEC] * 7 + [ANY_SPEC] * 2 + [VMEM_SPEC] * (2 + len(extra)),
        (FIRST_OUTS if first else [TURNED]) + [LATE],
        scratch(ACC, LOW, COEF) + [pltpu.SemaphoreType.DMA((2,))],
        (*scalars, vec, *tables, *every[8:], acc, low, *extra))
    return outs, (places, late)


def operator_full(first, scalars, vec, tables, dens, *extra):
    load = len(dens) > 2
    outs = FIRST_OUTS if first else [TURNED]
    dens = [d.reshape(-1, BS, L) for d in dens]
    return operator_call(
        functools.partial(full_kernel, first, len(dens)), "operator_full", 6_000_000_000,
        [SMEM_SPEC] * 5 + [VMEM_SPEC] * 7 + [ANY_SPEC if load else VMEM_SPEC] * len(dens) + [VMEM_SPEC] * len(extra),
        outs + [HALF_PLACES] * 2 if load else outs,
        scratch(ACC, LOW, COEF) + ([pltpu.SemaphoreType.DMA((len(dens),))] if load else []),
        (*scalars, vec, *tables, *dens, *extra))


def assemble_kernel(which, mine, got, out, sem):
    copies = []
    for k, ref in enumerate((mine, got)):
        half = which[0] if k == 0 else 1 - which[0]
        for part in range(2):
            copies.append(pltpu.make_async_copy(
                ref.at[part], out.at[part, pl.ds(pl.multiple_of(half * HALF, HALF), HALF)], sem.at[2 * k + part]))
    for copy in copies:
        copy.start()
    for copy in copies:
        copy.wait()


def assemble(which, mine, got):
    return pl.pallas_call(
        assemble_kernel,
        out_shape=jax.ShapeDtypeStruct((2, FB, 2 * BS), F32),
        in_specs=[SMEM_SPEC, VMEM_SPEC, VMEM_SPEC],
        out_specs=ANY_SPEC,
        scratch_shapes=[pltpu.SemaphoreType.DMA((4,))],
        compiler_params=pltpu.CompilerParams(vmem_limit_bytes=4 << 20),
        cost_estimate=pl.CostEstimate(flops=0, bytes_accessed=2 << 20, transcendentals=0),
        name="assemble",
    )(which, mine.reshape(2, HALF, 2 * BS), got.reshape(2, HALF, 2 * BS))


def index_of(y, x, core):
    return ((y % 4) * 4 + x % 4) * 2 + core


def step_pairs(stage, shift):
    pairs = []
    for y in range(4):
        for x in range(4):
            for core in range(2):
                along_x = (stage == 0) == (core == 0)
                target = index_of(y, x + shift, core) if along_x else index_of(y + shift, x, core)
                pairs.append((index_of(y, x, core), target))
    return pairs


def shifted(v, stage, shift):
    return lax.ppermute(v, "rows", step_pairs(stage, shift))


def to_other_core(v):
    return lax.ppermute(v, "rows", [(i, i ^ 1) for i in range(N_ROWS)])


def first_step(v):
    return [v, shifted(v, 0, 1), shifted(v, 0, -1), shifted(v, 0, 2)]


def second_step(parts):
    n = parts[0].shape[0]
    line = join(parts)
    line_before, line_after = shifted(line, 1, 1), shifted(line, 1, -1)
    across_lo = shifted(line_before[:2 * n], 1, 1)
    across_hi = shifted(line_after[2 * n:], 1, -1)
    return [line, line_before, line_after, across_lo, across_hi]


def body(consts, histories, shift_real, shift_imag, near_tiles, near_columns, left_factors,
         column_factor_tiles, tile_rows, tile_cols, tile_counts):
    hi, lo = consts
    me = lax.axis_index("rows")
    core, x0, y0 = me % 2, (me // 2) % 4, me // 8

    def own_half(s):
        return jnp.where(core == 0, s[:HALF], s[HALF:])

    shift_r, shift_i = own_half(shift_real), own_half(shift_imag)
    modulus = shift_r * shift_r + shift_i * shift_i
    inv_r, inv_i = shift_r / modulus, shift_i / modulus
    vec = jnp.stack([
        jnp.concatenate([inv_r, inv_r]),
        jnp.concatenate([inv_i, -inv_i]),
        jnp.concatenate([shift_r, shift_r]),
        jnp.concatenate([-shift_i, shift_i]),
    ])

    place_of = jnp.array([0, 2, 3, 1], jnp.int32)
    clusters = jnp.arange(BLOCKS, dtype=jnp.int32)
    to_x, to_y = place_of[(clusters // 4 - x0) % 4], place_of[(clusters // 16 - y0) % 4]
    chip_place = jnp.where(core == 0, to_y * 4 + to_x, to_x * 4 + to_y)
    pos = ((((clusters // 2) % 2) ^ core) * CHIPS + chip_place) * 2 + clusters % 2
    near = near_tiles.reshape(2 * NEAR, BS, BS)
    colf = column_factor_tiles.reshape(SLOTS_HERE * RANK, BS)
    left = left_factors.reshape(SLOTS_HERE * RANK, BS)
    whole = jnp.concatenate([near_columns.reshape(-1), tile_cols, tile_rows - me * 2, tile_counts])
    spectra, left_late = lax.optimization_barrier((spectrum(histories[0], hi, lo), left))
    left_t = turn(left_late)
    pieces = lax.all_to_all(
        spectra.reshape(N_FREQ * N_ROWS, 16, L), ("freq", "rows"), split_axis=0, concat_axis=0, tiled=True)
    whole_s = to_other_core(whole)
    near_s, colf_s, left_s = to_other_core(near), to_other_core(colf), to_other_core(left)
    tables_other = (near_s, colf_s, turn(left_s))
    pieces, whole_s, tables_other, left_t = lax.optimization_barrier((pieces, whole_s, tables_other, left_t))
    tables_own = (*(near[4 * g:4 * g + 4] for g in range(4)), colf, left_t)
    spec, spec_s = regroup(core.reshape(1), pieces)
    every = second_step(first_step(spec)) + second_step(first_step(spec_s))

    def scalars_of(w):
        return (w[:16], w[16:80], w[80:144], w[144:145], pos)

    scalars, scalars_s = scalars_of(whole), scalars_of(whole_s)

    corr, res, sol, *dens = operator_full(True, scalars, vec, tables_own, every, spec)
    corr, *tables_other = lax.optimization_barrier((corr, *tables_other))
    tables_other = stage(tables_other)
    corr_s, res_s, sol_s = operator_full(True, scalars_s, vec, tables_other, dens, spec_s)
    every = second_step(first_step(corr)) + second_step(first_step(corr_s))
    sol_got = to_other_core(sol_s)
    (resid_s,), dens = operator_split(False, scalars_s, vec, tables_other, every, corr_s, res_s)
    resid_got = to_other_core(resid_s)
    (resid,) = operator_full(False, scalars, vec, tables_own, dens, corr, res)

    which = core.reshape(1)
    return assemble(which, sol, sol_got), assemble(which, resid, resid_got)


def solution(mesh):
    hi, lo = tables()
    placed = (
        P(("freq", "rows"), None, None),
        P("freq"),
        P("freq"),
        P("freq", "rows", None, None, None),
        P("rows", None),
        P("freq", "rows", None, None),
        P("freq", "rows", None, None),
        P("rows"),
        P("rows"),
        P("rows"),
    )

    def run(*args):
        consts = tuple(jnp.asarray(c) for c in (hi, lo))
        return jax.shard_map(
            body,
            mesh=mesh,
            in_specs=((P(), P()),) + placed,
            out_specs=(P(None, "freq", "rows"), P(None, "freq", "rows")),
            check_vma=False,
        )(consts, *args)

    return run
```
